32 devices in a mesh: groups: 2 (over y), sub: 4 (over z), blk: 2 (over x), rep: 2 (over core).
Axes of the slice: x: 2, y: 2, z: 4, core: 2. Of those that a mesh axis runs over, the one named last changes fastest.
Arguments:
- collocation_locations: float32 [3, 4096], P(None, ('groups', 'sub', 'blk', 'rep')), parts along dimension 1, may hold values from 0 to 8, as said below
- source: float32 [4096], P(('groups', 'sub', 'blk', 'rep')), parts along dimension 0, may hold values from -6 to 6
- propagation_velocity_square: float32 [4096], P(('groups', 'sub', 'blk', 'rep')), parts along dimension 0, may hold values from 0.5 to 2
- live_count: int32 [32], P(('groups', 'sub', 'blk', 'rep')), parts along dimension 0, may hold values from 42 to 128, as said below
- intersection_index: int32 [2, 1024], P(None, ('groups', 'sub', 'blk', 'rep')), parts along dimension 1, may hold values from -1 to 127, as said below
- fine_hidden_matrices: bfloat16 [8, 256, 256], P('sub'), may hold values from -0.375 to 0.375
- fine_edge: bfloat16 [8, 6, 256], P('sub'), may hold values from -4 to 4
- coarse_hidden: bfloat16 [4, 256, 256], P('blk'), may hold values from -0.375 to 0.375
- coarse_edge: bfloat16 [4, 6, 256], P('blk'), may hold values from -4 to 4
Outputs:
- residual: float32 [4096], P(('groups', 'sub', 'blk', 'rep')), parts along dimension 0
- fine_grad_hidden: float32 [16, 256, 256], P(('groups', 'sub')), parts along dimension 0
- fine_grad_edge: float32 [16, 6, 256], P(('groups', 'sub')), parts along dimension 0
- coarse_grad_hidden: float32 [8, 256, 256], P(('groups', 'blk')), parts along dimension 0
- coarse_grad_edge: float32 [8, 6, 256], P(('groups', 'blk')), parts along dimension 0
- mean_loss: float32 [2], P('groups'), parts along dimension 0
The draws below stay inside these ranges and needn't reach their ends.
There are 2 independent parts, one for each index of `groups`. The reference program is written for one: setup_inputs(seed, part) draws one part's arguments, and reference() takes and returns one part's arrays. A program takes and returns all parts, laid end to end along the dimension named above; an argument that names none is the same for every part. Nothing has to cross between parts.
Inputs may be any that keep to these rules, and one draw needn't show every extreme that they name: The first live_count[q] slots of block q hold live points; some block is full. `intersection_index`: for each block, row 0 lists distinct live slots whose points lie in the intersection of the last fine subdomain of the slab on the left (periodically), row 1 those of the first fine subdomain of the slab on the right; used entries come first, then -1; at most 32 used entries per row and block, and some block fills both rows; no slot is in both rows. `collocation_locations`: time and the second space coordinate lie in [0, 1); the first space coordinate of a block of slab s lies in [s * 2, (s + 1) * 2).
All inputs are finite; a program needn't handle non-finite values.
Results may differ from the reference program's by a relative error of at most 0.0033.
Values may be sent and summed in bfloat16 or wider, within the bound.
A program may use at most 64 MiB of HBM per device.

```python
import math
import jax
import jax.numpy as jnp
from jax import lax

H = 256
FINE_DEV = 2
P_DEV = 128
CAP = 32
FINE = 8
COARSE = 4
BLOCKS = 16
POINTS = 2048
N_SUB = 4
N_BLK = 2
N_REP = 2


def layout(key):
    key_jitter, key_top, key_left, key_right, key_order = jax.random.split(key, 5)
    block_ids = jnp.arange(BLOCKS, dtype=jnp.int32)
    slab_ids = block_ids // (N_BLK * N_REP)
    low_count = P_DEV // 3
    rising = low_count + (P_DEV - low_count) * slab_ids // max(N_SUB - 1, 1)
    jitter = jax.random.randint(key_jitter, (BLOCKS,), 0, P_DEV // 8 + 1)
    counts = jnp.maximum(low_count, rising - jitter)
    top_block = jax.random.randint(key_top, (), 0, N_BLK * N_REP) + (N_SUB - 1) * N_BLK * N_REP
    counts = counts.at[top_block].set(P_DEV)
    halves = counts // 2
    left_len = jnp.minimum(jax.random.randint(key_left, (BLOCKS,), CAP // 4, CAP + 1), halves)
    right_len = jnp.minimum(jax.random.randint(key_right, (BLOCKS,), CAP // 4, CAP + 1), halves)
    left_len = left_len.at[top_block].set(CAP)
    right_len = right_len.at[top_block].set(CAP)
    positions = jnp.arange(P_DEV, dtype=jnp.int32)
    scores = jax.random.randint(key_order, (BLOCKS, P_DEV), 0, P_DEV) * P_DEV + positions[None, :]
    scores = scores + (positions[None, :] >= counts[:, None]).astype(jnp.int32) * (P_DEV * P_DEV)
    order = jnp.argsort(scores, axis=1, stable=True).astype(jnp.int32)
    ranks = jnp.argsort(order, axis=1, stable=True).astype(jnp.int32)
    return (counts, left_len, right_len, order, ranks)


def draw_live_count(key, part):
    counts, left_len, right_len, order, ranks = layout(key)
    return counts


def draw_intersection_index(key, part):
    counts, left_len, right_len, order, ranks = layout(key)
    slot_ids = jnp.arange(CAP, dtype=jnp.int32)[None, :]
    left_rows = jnp.where(slot_ids < left_len[:, None], order[:, :CAP], -1)
    right_take = jnp.clip(left_len[:, None] + slot_ids, 0, P_DEV - 1)
    right_rows = jnp.where(slot_ids < right_len[:, None], jnp.take_along_axis(order, right_take, axis=1), -1)
    return jnp.stack([left_rows, right_rows]).reshape(2, BLOCKS * CAP).astype(jnp.int32)


def draw_collocation_locations(key, part):
    counts, left_len, right_len, order, ranks = layout(key)
    key = jax.random.fold_in(key, 11)
    key_place, key_time, key_space = jax.random.split(key, 3)
    uniform_draw = jax.random.uniform(key_place, (BLOCKS, P_DEV), jnp.float32)
    layer_start_moment = (jnp.arange(BLOCKS, dtype=jnp.int32) // (N_BLK * N_REP) * FINE_DEV).astype(jnp.float32)[:, None]
    position_locations = jnp.where(ranks < left_len[:, None], layer_start_moment + 0.5 * uniform_draw, jnp.where(ranks < (left_len + right_len)[:, None], layer_start_moment + (FINE_DEV - 0.5) + 0.5 * uniform_draw, jnp.where(ranks < counts[:, None], layer_start_moment + 0.5 + (FINE_DEV - 1) * uniform_draw, layer_start_moment + FINE_DEV * uniform_draw)))
    temporal_random_pick = jax.random.uniform(key_time, (BLOCKS, P_DEV), jnp.float32)
    space_draw = jax.random.uniform(key_space, (BLOCKS, P_DEV), jnp.float32)
    temporal_moments = temporal_random_pick
    position_vectors = space_draw
    position_locations = jnp.minimum(position_locations, layer_start_moment + (FINE_DEV - 0.0001))
    return jnp.stack([temporal_moments.reshape(-1), position_locations.reshape(-1), position_vectors.reshape(-1)]).astype(jnp.float32)


def block_levels(stream_key, shape, cuts, smallest, top_value):
    level = 1.0
    for axis_at, parts in cuts:
        heights = jax.random.uniform(jax.random.fold_in(jax.random.fold_in(stream_key, 6), axis_at), (parts,), jnp.float32, smallest / len(cuts), top_value / len(cuts))
        level = level * jnp.repeat(jnp.exp(heights), shape[axis_at] // parts).reshape((-1,) + (1,) * (len(shape) - 1 - axis_at))
    return level


def bell_draw(key, dims, spread, bound, cuts=(), held_as=jnp.bfloat16):
    array = spread * jax.random.normal(key, dims, jnp.float32)
    if cuts:
        array = array * block_levels(key, dims, cuts, -0.22, 0.18)
    return jnp.clip(array, -bound, bound).astype(held_as)


def setup_inputs(seed: int = 0, part: int = 0) -> dict:
    streams_of = jax.random.split(jax.random.key(seed), 10)
    part_keys = jax.random.split(jax.random.fold_in(streams_of[9], part), 10)
    collocation_locations = draw_collocation_locations(jax.random.fold_in(jax.random.fold_in(streams_of[9], part), 71), part)
    source = bell_draw(part_keys[1], (POINTS,), 1.0, 6.0, ((0, 16),), jnp.float32)
    propagation_velocity_square = jnp.clip(jnp.exp(math.log(2.0) - 1.3862944 * jax.random.uniform(part_keys[2], (POINTS,), jnp.float32) ** block_levels(part_keys[2], (POINTS,), ((0, 16),), -0.2, 0.2)), 0.5, 2.0)
    live_count = draw_live_count(jax.random.fold_in(jax.random.fold_in(streams_of[9], part), 71), part)
    intersection_index = draw_intersection_index(jax.random.fold_in(jax.random.fold_in(streams_of[9], part), 71), part)
    fine_hidden_matrices = bell_draw(streams_of[5], (FINE, H, H), H ** -0.5, 0.375, ((0, 4),))
    fine_edge = bell_draw(streams_of[6], (FINE, 6, H), 1.0, 4.0, ((0, 4),))
    coarse_hidden = bell_draw(streams_of[7], (COARSE, H, H), H ** -0.5, 0.375, ((0, 2),))
    coarse_edge = bell_draw(streams_of[8], (COARSE, 6, H), 1.0, 4.0, ((0, 2),))
    return {"collocation_locations": collocation_locations, "source": source, "propagation_velocity_square": propagation_velocity_square, "live_count": live_count, "intersection_index": intersection_index, "fine_hidden_matrices": fine_hidden_matrices, "fine_edge": fine_edge, "coarse_hidden": coarse_hidden, "coarse_edge": coarse_edge}


window_width_sq = 0.36
residual_scale = 0.125
fine_factors = (2.0, 2.0, 2.0)

def first_layer(boundary_rows, learner_arguments, unity_multipliers):
    weights_in = boundary_rows[0:3]
    bias_in = boundary_rows[3]
    preact = learner_arguments[0][:, None] * weights_in[0] + learner_arguments[1][:, None] * weights_in[1] + learner_arguments[2][:, None] * weights_in[2] + bias_in
    active = jnp.tanh(preact)
    slopes = 1.0 - active * active
    firsts = [slopes * (unity_multipliers[axis_id] * weights_in[axis_id]) for axis_id in range(3)]
    seconds = [-2.0 * active * slopes * (unity_multipliers[axis_id] * weights_in[axis_id]) ** 2 for axis_id in range(3)]
    return jnp.stack([active] + firsts + seconds)

def second_layer(streams, boundary_rows, unity_bump, wave_speeds):
    bias_mid = boundary_rows[4]
    weights_out = boundary_rows[5] / jnp.sqrt(jnp.float32(boundary_rows.shape[1]))
    active = jnp.tanh(streams[0] + bias_mid)
    slopes = 1.0 - active * active
    net_value = lax.optimization_barrier(jnp.sum(active * weights_out, axis=-1))
    slope_x = lax.optimization_barrier(jnp.sum(slopes * streams[2] * weights_out, axis=-1))
    curvature = [lax.optimization_barrier(jnp.sum((slopes * streams[4 + axis_id] - 2.0 * active * slopes * streams[1 + axis_id] ** 2) * weights_out, axis=-1)) for axis_id in range(3)]
    weight, weight_x, weight_xx = unity_bump
    return weight * curvature[0] - wave_speeds * (weight_xx * net_value + 2.0 * weight_x * slope_x + weight * curvature[1] + weight * curvature[2])

def net_forward(hidden_activations, boundary_rows, learner_arguments, unity_multipliers, unity_bump, wave_speeds):
    streams = first_layer(boundary_rows, learner_arguments, unity_multipliers)
    rounded = streams.astype(jnp.bfloat16)
    rows_total = streams.shape[0] * streams.shape[1]
    columns = streams.shape[2]
    layer_in = jnp.dot(rounded.reshape(rows_total, columns), hidden_activations, preferred_element_type=jnp.float32).reshape(streams.shape)
    return (second_layer(layer_in, boundary_rows, unity_bump, wave_speeds), rounded, layer_in)

def net_backward(hidden_activations, boundary_rows, learner_arguments, unity_multipliers, unity_bump, wave_speeds, rounded, layer_in, cotangent):
    _, back_out = jax.vjp(lambda arg_streams, arg_edges: second_layer(arg_streams, arg_edges, unity_bump, wave_speeds), layer_in, boundary_rows)
    grad_streams, grad_edge_out = back_out(cotangent)
    rows_total = rounded.shape[0] * rounded.shape[1]
    columns = rounded.shape[2]
    grad_low = grad_streams.astype(jnp.bfloat16).reshape(rows_total, columns)
    flat_streams = rounded.reshape(rows_total, columns)
    grad_hidden = lax.dot_general(flat_streams, grad_low, (((0,), (0,)), ((), ())), preferred_element_type=jnp.float32)
    grad_inputs = lax.dot_general(grad_low, hidden_activations, (((1,), (1,)), ((), ())), preferred_element_type=jnp.float32).reshape(rounded.shape)
    _, back_in = jax.vjp(lambda arg_edges: first_layer(arg_edges, learner_arguments, unity_multipliers), boundary_rows)
    grad_edge_in, = back_in(grad_inputs)
    return (grad_hidden, grad_edge_out + grad_edge_in)

def window_of(displacement_amounts, width_sq):
    weight = jnp.exp(-displacement_amounts * displacement_amounts / width_sq)
    weight_x = -2.0 * displacement_amounts / width_sq * weight
    weight_xx = (4.0 * displacement_amounts * displacement_amounts / (width_sq * width_sq) - 2.0 / width_sq) * weight
    return (weight, weight_x, weight_xx)

def detailed_level_arrangement(temporal_moments, displacement_amounts, position_vectors):
    learner_arguments = jnp.stack([2.0 * (temporal_moments - 0.5), 2.0 * displacement_amounts, 2.0 * (position_vectors - 0.5)])
    return (learner_arguments, window_of(displacement_amounts, window_width_sq))

def rough_level_arrangement(temporal_moments, displacement_amounts, position_vectors, bump_halfwidth):
    learner_arguments = jnp.stack([2.0 * (temporal_moments - 0.5), 2.0 * displacement_amounts / bump_halfwidth, 2.0 * (position_vectors - 0.5)])
    unity_multipliers = (2.0, 2.0 / bump_halfwidth, 2.0)
    return (learner_arguments, window_of(displacement_amounts, window_width_sq * bump_halfwidth * bump_halfwidth), unity_multipliers)

def reference(collocation_locations, source, propagation_velocity_square, live_count, intersection_index, fine_hidden_matrices, fine_edge, coarse_hidden, coarse_edge):
    fine_total = FINE_DEV * N_SUB
    per_slab = N_BLK * N_REP
    slabs_per_cell = N_SUB // COARSE
    bump_halfwidth = fine_total / COARSE
    columns = fine_hidden_matrices.shape[1]
    coord_blocks = collocation_locations.reshape(3, BLOCKS, P_DEV).transpose(1, 0, 2)
    source_blocks = source.reshape(BLOCKS, P_DEV)
    speed_blocks = propagation_velocity_square.reshape(BLOCKS, P_DEV)
    index_blocks = intersection_index.reshape(2, BLOCKS, CAP).transpose(1, 0, 2)
    fine_boundary_weights = fine_edge.astype(jnp.float32)
    coarse_edges = coarse_edge.astype(jnp.float32)
    positions = jnp.arange(P_DEV, dtype=jnp.int32)

    def step_block(carried, blocks_in):
        grad_fh, grad_fe, grad_ch, grad_ce, square_sum, live_sum = carried
        block_id, collocation_nodes, sources, wave_speeds, live_here, indices = blocks_in
        slab_id = block_id // per_slab
        cell_id = slab_id // slabs_per_cell
        layer_start_moment = slab_id.astype(jnp.float32) * FINE_DEV
        temporal_moments, position_locations, position_vectors = (collocation_nodes[0], collocation_nodes[1], collocation_nodes[2])
        live_mask = (positions < live_here).astype(jnp.float32)
        totals = jnp.zeros((P_DEV,), jnp.float32)
        fine_runs = []
        for piecewise_learner in range(FINE_DEV):
            net_id = slab_id * FINE_DEV + piecewise_learner
            learner_arguments, unity_bump = detailed_level_arrangement(temporal_moments, position_locations - (layer_start_moment + (piecewise_learner + 0.5)), position_vectors)
            contrib, rounded, layer_in = net_forward(fine_hidden_matrices[net_id], fine_boundary_weights[net_id], learner_arguments, fine_factors, unity_bump, wave_speeds)
            totals = totals + contrib
            fine_runs.append((net_id, learner_arguments, unity_bump, wave_speeds, rounded, layer_in))
        coarse_runs = []
        for shift_id in range(3):
            coarse_id = (cell_id + (shift_id - 1)) % COARSE
            region_centroid = (cell_id.astype(jnp.float32) + (shift_id - 0.5)) * bump_halfwidth
            learner_arguments, unity_bump, unity_multipliers = rough_level_arrangement(temporal_moments, position_locations - region_centroid, position_vectors, bump_halfwidth)
            contrib, rounded, layer_in = net_forward(coarse_hidden[coarse_id], coarse_edges[coarse_id], learner_arguments, unity_multipliers, unity_bump, wave_speeds)
            totals = totals + contrib
            coarse_runs.append((coarse_id, learner_arguments, unity_bump, unity_multipliers, rounded, layer_in))
        remote_runs = []
        for side_id in range(2):
            if side_id == 0:
                net_id = (slab_id * FINE_DEV - 1) % fine_total
                bump_centroid = layer_start_moment - 0.5
            else:
                net_id = (slab_id + 1) * FINE_DEV % fine_total
                bump_centroid = layer_start_moment + (FINE_DEV + 0.5)
            bounded_position = jnp.maximum(indices[side_id], 0)
            valid_mask = (indices[side_id] >= 0).astype(jnp.float32)
            learner_arguments, unity_bump = detailed_level_arrangement(temporal_moments[bounded_position], position_locations[bounded_position] - bump_centroid, position_vectors[bounded_position])
            listed_speeds = wave_speeds[bounded_position]
            contrib, rounded, layer_in = net_forward(fine_hidden_matrices[net_id], fine_boundary_weights[net_id], learner_arguments, fine_factors, unity_bump, listed_speeds)
            totals = totals.at[bounded_position].add(contrib * valid_mask)
            remote_runs.append((net_id, learner_arguments, unity_bump, listed_speeds, rounded, layer_in, bounded_position, valid_mask))
        residuals = (totals * residual_scale - sources) * live_mask
        cotangent = residuals * residual_scale
        for net_id, learner_arguments, unity_bump, run_speeds, rounded, layer_in in fine_runs:
            grad_hidden, grad_edges = net_backward(fine_hidden_matrices[net_id], fine_boundary_weights[net_id], learner_arguments, fine_factors, unity_bump, run_speeds, rounded, layer_in, cotangent)
            grad_fh = grad_fh.at[net_id].add(grad_hidden)
            grad_fe = grad_fe.at[net_id].add(grad_edges)
        for coarse_id, learner_arguments, unity_bump, unity_multipliers, rounded, layer_in in coarse_runs:
            grad_hidden, grad_edges = net_backward(coarse_hidden[coarse_id], coarse_edges[coarse_id], learner_arguments, unity_multipliers, unity_bump, wave_speeds, rounded, layer_in, cotangent)
            grad_ch = grad_ch.at[coarse_id].add(grad_hidden)
            grad_ce = grad_ce.at[coarse_id].add(grad_edges)
        for net_id, learner_arguments, unity_bump, run_speeds, rounded, layer_in, bounded_position, valid_mask in remote_runs:
            grad_hidden, grad_edges = net_backward(fine_hidden_matrices[net_id], fine_boundary_weights[net_id], learner_arguments, fine_factors, unity_bump, run_speeds, rounded, layer_in, cotangent[bounded_position] * valid_mask)
            grad_fh = grad_fh.at[net_id].add(grad_hidden)
            grad_fe = grad_fe.at[net_id].add(grad_edges)
        square_sum = square_sum + jnp.sum(residuals * residuals)
        live_sum = live_sum + live_here.astype(jnp.float32)
        return ((grad_fh, grad_fe, grad_ch, grad_ce, square_sum, live_sum), residuals)
    initial = (jnp.zeros((FINE, columns, columns), jnp.float32), jnp.zeros((FINE, 6, columns), jnp.float32), jnp.zeros((COARSE, columns, columns), jnp.float32), jnp.zeros((COARSE, 6, columns), jnp.float32), jnp.zeros((), jnp.float32), jnp.zeros((), jnp.float32))
    blocks_in = (jnp.arange(BLOCKS, dtype=jnp.int32), coord_blocks, source_blocks, speed_blocks, live_count, index_blocks)
    carried, residuals = lax.scan(step_block, initial, blocks_in)
    mean_loss = (carried[4] / carried[5]).reshape(1)
    return (residuals.reshape(POINTS), carried[0], carried[1], carried[2], carried[3], mean_loss)
```

```python
import functools

import jax
import jax.numpy as jnp
from jax import lax
from jax.experimental import pallas as pl
from jax.experimental.pallas import tpu as pltpu
from jax.sharding import PartitionSpec as P

MESH = pl.DeviceIdType.MESH
F32 = jnp.float32
BF16 = jnp.bfloat16
WIDTH_SQ = 0.36
CHUNK = 16
UNROLL = 2
EXACT = lax.Precision.HIGHEST


def wide(tile, columns):
    return jnp.concatenate([tile] * (columns // tile.shape[1]), axis=1)


def fold(value):
    total = value[0:8]
    for at in range(8, value.shape[0], 8):
        total = total + value[at : at + 8]
    return total


def rows_of(step):
    return pl.ds(pl.multiple_of(step * CHUNK, CHUNK), CHUNK)


def window_rows(dx, width_sq, speed):
    weight = jnp.exp(-dx * dx / width_sq)
    weight_x = -2.0 * dx / width_sq * weight
    weight_xx = (4.0 * dx * dx / (width_sq * width_sq) - 2.0 / width_sq) * weight
    return (weight, speed * weight, 2.0 * speed * weight_x, speed * weight_xx)


class Net:
    def __init__(self, count, factors, edge, weights, cols, offset, ids, streams, layers, hidden):
        self.count, self.factors = count, factors
        self.edge, self.weights = edge, weights
        self.cols, self.offset, self.ids = cols, offset, ids
        self.streams, self.layers, self.hidden = streams, layers, hidden

    def col(self, name, step):
        at = self.ids[name]
        rows = pl.ds(pl.multiple_of(self.offset + step * CHUNK, CHUNK), CHUNK)
        return self.cols[rows, at : at + 1]

    def forward(self, totals):
        edge = self.edge()
        e = [edge[j : j + 1] for j in range(6)]
        columns = edge.shape[1]
        scaled = [self.factors[d] * e[d] for d in range(3)]
        squares = [s * s for s in scaled]

        def first(step, carry):
            rows = rows_of(step)
            pre = (
                self.col("t", step) * e[0]
                + self.col("x", step) * e[1]
                + self.col("y", step) * e[2]
                + e[3]
            )
            h = jnp.tanh(pre)
            g = 1.0 - h * h
            s = -2.0 * h * g
            self.hidden[rows, :] = h
            self.streams[0, rows, :] = h.astype(BF16)
            for d in range(3):
                self.streams[1 + d, rows, :] = (g * scaled[d]).astype(BF16)
                self.streams[4 + d, rows, :] = (s * squares[d]).astype(BF16)
            return carry

        steps = self.count // CHUNK
        lax.fori_loop(0, steps, first, 0, unroll=UNROLL)
        flat = self.streams[...].reshape(7 * self.count, columns)
        self.layers[...] = jnp.dot(
            flat, self.weights(), preferred_element_type=F32
        ).reshape(7, self.count, columns)
        out = e[5] * (1.0 / float(columns) ** 0.5)

        def second(step, carry):
            rows = rows_of(step)
            w, cw = self.col("w", step), self.col("cw", step)
            cx, cxx = self.col("cx", step), self.col("cxx", step)
            k = jnp.tanh(self.layers[0, rows, :] + e[4])
            m = 1.0 - k * k
            l1, l2, l3 = [self.layers[j, rows, :] for j in (1, 2, 3)]
            curved = (
                w * self.layers[4, rows, :]
                - cw * (self.layers[5, rows, :] + self.layers[6, rows, :])
                - cx * l2
            )
            q = w * (l1 * l1) - cw * (l2 * l2 + l3 * l3)
            v = curved - 2.0 * k * q
            t = m * v - cxx * k
            self.layers[0, rows, :] = k
            self.layers[4, rows, :] = v
            self.layers[5, rows, :] = q
            self.layers[6, rows, :] = t
            value = jnp.sum(t * out, axis=1, keepdims=True)
            at = pl.ds(pl.multiple_of(self.offset + step * CHUNK, CHUNK), CHUNK)
            totals[at, :] = totals[at, :] + jnp.broadcast_to(value, (CHUNK, 128))
            return carry

        lax.fori_loop(0, steps, second, 0, unroll=UNROLL)

    def backward(self, cotangent, grads, grad_out, edge_out):
        edge = self.edge()
        e = [edge[j : j + 1] for j in range(6)]
        columns = edge.shape[1]
        norm = 1.0 / float(columns) ** 0.5
        out = e[5] * norm
        scaled = [self.factors[d] * e[d] for d in range(3)]
        squares = [s * s for s in scaled]
        zero = jnp.zeros((8, columns), F32)
        steps = self.count // CHUNK
        low = grads.at[:, pl.ds(0, self.count), :]

        def first(step, carry):
            rows = rows_of(step)
            at = pl.ds(pl.multiple_of(self.offset + step * CHUNK, CHUNK), CHUNK)
            cot = wide(cotangent[at, :], columns)
            w, cw = self.col("w", step), self.col("cw", step)
            cx, cxx = self.col("cx", step), self.col("cxx", step)
            k, l1, l2, l3, v, q, t = [self.layers[j, rows, :] for j in range(7)]
            m = 1.0 - k * k
            com = cot * out * m
            k4 = 4.0 * k * com
            kc = k4 * cw
            g0 = com * (-2.0 * (k * v + m * q) - cxx)
            low[0, rows, :] = g0.astype(BF16)
            low[1, rows, :] = (-(k4 * w) * l1).astype(BF16)
            low[2, rows, :] = (kc * l2 - com * cx).astype(BF16)
            low[3, rows, :] = (kc * l3).astype(BF16)
            low[4, rows, :] = (com * w).astype(BF16)
            minus = (-(com * cw)).astype(BF16)
            low[5, rows, :] = minus
            low[6, rows, :] = minus
            return (carry[0] + fold(g0), carry[1] + fold(cot * t))

        sum4, sum5 = lax.fori_loop(0, steps, first, (zero, zero), unroll=UNROLL)
        flat = self.streams[...].reshape(7 * self.count, columns)
        flat_low = low[...].reshape(7 * self.count, columns)
        grad_out(
            lax.dot_general(
                flat, flat_low, (((0,), (0,)), ((), ())), preferred_element_type=F32
            )
        )
        self.layers[...] = lax.dot_general(
            flat_low, self.weights(), (((1,), (1,)), ((), ())), preferred_element_type=F32
        ).reshape(7, self.count, columns)

        def second(step, carry):
            rows = rows_of(step)
            h = self.hidden[rows, :]
            i = [self.layers[j, rows, :] for j in range(7)]
            h2 = h * h
            g = 1.0 - h2
            s = -2.0 * h * g
            lin = i[1] * scaled[0] + i[2] * scaled[1] + i[3] * scaled[2]
            quad = i[4] * squares[0] + i[5] * squares[1] + i[6] * squares[2]
            da = g * (i[0] - 2.0 * h * lin + (6.0 * h2 - 2.0) * quad)
            terms = [
                da,
                da * self.col("t", step),
                da * self.col("x", step),
                da * self.col("y", step),
            ]
            terms += [g * i[1 + d] for d in range(3)] + [s * i[4 + d] for d in range(3)]
            return tuple(c + fold(x) for c, x in zip(carry, terms))

        sums = lax.fori_loop(0, steps, second, (zero,) * 10, unroll=UNROLL)
        sums = [jnp.sum(x, axis=0, keepdims=True) for x in sums]
        rows = [
            sums[1 + d]
            + self.factors[d] * sums[4 + d]
            + 2.0 * self.factors[d] * scaled[d] * sums[7 + d]
            for d in range(3)
        ]
        rows.append(sums[0])
        rows.append(jnp.sum(sum4, axis=0, keepdims=True))
        rows.append(jnp.sum(sum5, axis=0, keepdims=True) * norm)
        for j, row in enumerate(rows):
            edge_out(j, row)


def kernel(
    S, B, CB, FD, points_ref, source_ref, speed_ref, live_ref, index_ref, fh_ref, fe_ref, ch_ref,
    ce_ref, res_out, fgh_out, fge_out, cgh_out, cge_out, loss_out,
    call, cedge, fedge, wl, wr, edge_l, edge_r, rows_sc, cols, lrows, lcols, pick_t, pick,
    totals, ltotals, cot, lcot, idx_sc, st, layers, hid, stl, ll, hl, grads,
    gh, gr, cge, cge_r, lge, lge_r, fge, fge_r,
    cown, cst, cxr, csum, zst, zr, zg, zg2, cex, cez, fown, fst, fxr, nst, nz, lex, lez, fex,
    fag, fg, fg2,
    w_send, w_recv, chip_send, chip_recv, x_send, x_recv, z_send, z_recv, a_send, a_recv,
):
    C = CB * B
    PS = S // CB
    NP = points_ref.shape[1]
    cap = index_ref.shape[1]
    H = fh_ref.shape[1]
    s, b, r = lax.axis_index("sub"), lax.axis_index("blk"), lax.axis_index("rep")
    other = 1 - r
    right, left = lax.rem(s + 1, S), lax.rem(s + S - 1, S)
    cell = s // max(S // C, 1)
    half_width = float(FD * S) / float(C)

    barrier = pltpu.get_barrier_semaphore()
    pl.semaphore_signal(barrier, inc=1, device_id={"rep": other}, device_id_type=MESH)
    for d in range(1, B):
        pl.semaphore_signal(
            barrier, inc=1, device_id={"blk": lax.rem(b + d, B)}, device_id_type=MESH
        )
    for d in range(1, S):
        pl.semaphore_signal(
            barrier, inc=1, device_id={"sub": lax.rem(s + d, S)}, device_id_type=MESH
        )

    fedge[...] = jnp.zeros_like(fedge)
    for k in range(FD):
        fedge[k, 0:6, :] = fe_ref[k].astype(F32)
    for k in range(CB):
        cedge[b * CB + k] = jnp.concatenate(
            [ce_ref[k].astype(F32), jnp.zeros((2, H), F32)], axis=0
        )
        call[b * CB + k] = ch_ref[k]
    pl.semaphore_wait(barrier, S + B - 1)

    def remote(src, dst, send, recv, **where):
        copy = pltpu.make_async_remote_copy(
            src_ref=src, dst_ref=dst, send_sem=send, recv_sem=recv,
            device_id=where, device_id_type=MESH,
        )
        copy.start()
        return copy

    wcopies = [
        remote(fh_ref.at[0], wr, w_send.at[0], w_recv.at[0], sub=left),
        remote(fh_ref.at[FD - 1], wl, w_send.at[1], w_recv.at[1], sub=right),
        remote(fedge.at[0], edge_r, w_send.at[2], w_recv.at[2], sub=left),
        remote(fedge.at[FD - 1], edge_l, w_send.at[3], w_recv.at[3], sub=right),
    ]
    mine = pl.ds(b * CB, CB)
    xcopies = []
    for d in range(1, B):
        to = lax.rem(b + d, B)
        xcopies.append(
            remote(ch_ref, call.at[mine], w_send.at[2 + 2 * d], w_recv.at[2 + 2 * d], blk=to)
        )
        xcopies.append(
            remote(
                cedge.at[mine], cedge.at[mine], w_send.at[3 + 2 * d], w_recv.at[3 + 2 * d], blk=to
            )
        )

    start = s.astype(F32) * FD
    t_row, x_row, y_row = points_ref[0:1, :], points_ref[1:2, :], points_ref[2:3, :]
    speed_row = speed_ref[...]
    rows_sc[...] = jnp.zeros_like(rows_sc)
    rows_sc[0:1, :] = 2.0 * (t_row - 0.5)
    rows_sc[1:2, :] = 2.0 * (y_row - 0.5)
    rows_sc[2:3, :] = source_ref[...]
    ids = []
    for e in range(FD + 3):
        if e < FD:
            dx = x_row - (start + (e + 0.5))
            width, z = WIDTH_SQ, 2.0 * dx
        else:
            dx = x_row - (cell.astype(F32) + (e - FD - 0.5)) * half_width
            width, z = WIDTH_SQ * half_width * half_width, 2.0 * dx / half_width
        at = 3 + 5 * e
        rows_sc[at : at + 1, :] = z
        for j, row in enumerate(window_rows(dx, width, speed_row)):
            rows_sc[at + 1 + j : at + 2 + j, :] = row
        ids.append({"t": 0, "y": 1, "x": at, "w": at + 1, "cw": at + 2, "cx": at + 3, "cxx": at + 4})
    cols[...] = rows_sc[...].T
    idx_sc[...] = jnp.full_like(idx_sc, -1)
    idx_sc[0:1, 0:cap] = index_ref[0:1, :]
    idx_sc[0:1, cap : 2 * cap] = index_ref[1:2, :]
    pick_t[...] = (
        lax.broadcasted_iota(jnp.int32, (NP, 128), 0) == idx_sc[0:1, :]
    ).astype(F32)
    pick[...] = pick_t[...].T
    fields = jnp.concatenate(
        [points_ref[...], speed_row, jnp.zeros((4, NP), F32)], axis=0
    )
    listed = jnp.dot(fields, pick_t[...], preferred_element_type=F32, precision=EXACT)
    is_left = lax.broadcasted_iota(jnp.int32, (1, 128), 1) < cap
    dx = listed[1:2] - jnp.where(is_left, start - 0.5, start + (FD + 0.5))
    lrows[...] = jnp.zeros_like(lrows)
    lrows[0:1, :] = 2.0 * (listed[0:1] - 0.5)
    lrows[1:2, :] = 2.0 * (listed[2:3] - 0.5)
    lrows[3:4, :] = 2.0 * dx
    for j, row in enumerate(window_rows(dx, WIDTH_SQ, listed[3:4])):
        lrows[4 + j : 5 + j, :] = row
    lcols[...] = lrows[...].T
    lids = ids[0]

    fine_f = (2.0, 2.0, 2.0)
    coarse_f = (2.0, 2.0 / half_width, 2.0)
    fine = [
        Net(NP, fine_f, lambda k=k: fedge[k], lambda k=k: fh_ref[k], cols, 0, ids[k],
            st.at[k], layers.at[k], hid.at[k])
        for k in range(FD)
    ]
    cids = [lax.rem(cell + (u + C - 1), C) for u in range(3)]
    coarse = [
        Net(NP, coarse_f, lambda u=u: cedge[cids[u]], lambda u=u: call[cids[u]], cols, 0,
            ids[FD + u], st.at[FD + u], layers.at[FD + u], hid.at[FD + u])
        for u in range(3)
    ]
    lists = [
        Net(cap, fine_f, lambda: edge_l[...], lambda: wl[...], lcols, 0, lids,
            stl.at[0], ll.at[0], hl.at[0]),
        Net(cap, fine_f, lambda: edge_r[...], lambda: wr[...], lcols, cap, lids,
            stl.at[1], ll.at[1], hl.at[1]),
    ]

    totals[...] = jnp.zeros_like(totals)
    ltotals[...] = jnp.zeros_like(ltotals)
    for net in fine:
        net.forward(totals)
    for copy in xcopies:
        copy.wait()
    for net in coarse:
        net.forward(totals)
    for copy in wcopies:
        copy.wait()
    for net in lists:
        net.forward(ltotals)

    total = totals[...] + jnp.dot(
        pick_t[...], ltotals[...], preferred_element_type=F32, precision=EXACT
    )
    count = live_ref[0]
    live = (lax.broadcasted_iota(jnp.int32, (NP, 128), 0) < count).astype(F32)
    residual = (total * 0.125 - cols[:, 2:3]) * live
    res_out[...] = residual.T[0:1, :]
    cot[...] = residual * 0.125
    lcot[...] = jnp.dot(pick[...], cot[...], preferred_element_type=F32, precision=EXACT)
    loss_row = wide(jnp.sum(residual * residual, axis=0, keepdims=True), H)
    count_row = jnp.full((1, H), 1.0, F32) * count.astype(F32)
    blank = jnp.concatenate([jnp.zeros((6, H), F32), loss_row, count_row], axis=0)
    for c in range(C):
        cge[c] = blank
    lge[...] = jnp.zeros_like(lge)
    fge[...] = jnp.zeros_like(fge)
    cown[...] = jnp.zeros_like(cown)
    cst[...] = jnp.zeros_like(cst)

    def run_back(e, net, cotangent, edge_ref, edge_at):
        def keep(value):
            gh[e] = value.reshape(gh.shape[1:])

        def keep_edge(j, row):
            edge_ref[edge_at, j : j + 1, :] = row

        net.backward(cotangent, grads, keep, keep_edge)
        return remote(
            gh.at[e, other], gr.at[e], chip_send.at[e], chip_recv.at[e], rep=other
        )

    NE = FD + 5
    chip = {}
    for u in range(3):
        chip[u] = run_back(u, coarse[u], cot, cge, cids[u])
    chip["ce"] = remote(cge, cge_r, chip_send.at[NE], chip_recv.at[NE], rep=other)
    for n in range(2):
        chip[3 + n] = run_back(3 + n, lists[n], lcot, lge, n)
    chip["le"] = remote(lge, lge_r, chip_send.at[NE + 1], chip_recv.at[NE + 1], rep=other)

    for u in range(3):
        chip[u].wait()
        value = (gh[u, r] + gr[u]).reshape(cown.shape[1:])
        cown[cids[u]] = value
        cst[cids[u]] = value.astype(cst.dtype)
    chip["ce"].wait()
    cge[...] = cge[...] + cge_r[...]
    cex[b] = cge[mine]
    cx = []
    for d in range(1, B):
        to = lax.rem(b + d, B)
        theirs = pl.ds(to * CB, CB)
        cx.append(
            remote(cst.at[theirs], cxr.at[b], x_send.at[d, 0], x_recv.at[d, 0], blk=to)
        )
        cx.append(
            remote(cge.at[theirs], cex.at[b], x_send.at[d, 1], x_recv.at[d, 1], blk=to)
        )

    chip[5] = run_back(5, fine[0], cot, fge, 0)

    def share(e, n):
        chip[e].wait()
        fown[n] = gh[e, r, b] + gr[e, b]
        for d in range(1, B):
            to = lax.rem(b + d, B)
            fst[to, n] = (gh[e, r, to] + gr[e, to]).astype(BF16)

    for n in range(2):
        share(3 + n, n)
    chip["le"].wait()
    lge[...] = lge[...] + lge_r[...]
    lex[b] = lge[...]
    lx = []
    for d in range(1, B):
        to = lax.rem(b + d, B)
        lx.append(
            remote(fst.at[to, pl.ds(0, 2)], fxr.at[b, pl.ds(0, 2)], x_send.at[d, 2],
                   x_recv.at[d, 2], blk=to)
        )
        lx.append(remote(lge, lex.at[b], x_send.at[d, 3], x_recv.at[d, 3], blk=to))

    for copy in cx:
        copy.wait()
    for k in range(CB):
        value = cown[b * CB + k]
        for d in range(1, B):
            value = value + cxr[lax.rem(b + d, B), k].astype(F32)
        csum[k] = value
        zst[k] = value.astype(zst.dtype)
    edge_sum = cex[0]
    for d in range(1, B):
        edge_sum = edge_sum + cex[d]
    cez[s] = edge_sum
    cz = []
    for d in range(1, S):
        to = lax.rem(s + d, S)
        cz.append(
            remote(zst.at[to // PS, lax.rem(to, PS)], zr.at[s], z_send.at[d, 0],
                   z_recv.at[d, 0], sub=to)
        )
        cz.append(remote(cez.at[s], cez.at[s], z_send.at[d, 1], z_recv.at[d, 1], sub=to))

    for k in range(1, FD):
        chip[5 + k] = run_back(5 + k, fine[k], cot, fge, k)
    chip["fe"] = remote(fge, fge_r, chip_send.at[NE + 2], chip_recv.at[NE + 2], rep=other)

    for copy in lx:
        copy.wait()
    for n in range(2):
        value = fown[n]
        for d in range(1, B):
            value = value + fxr[lax.rem(b + d, B), n].astype(F32)
        nst[n] = value.astype(BF16)
    edge_sum = lex[0]
    for d in range(1, B):
        edge_sum = edge_sum + lex[d]
    lge[...] = edge_sum
    nx = [
        remote(nst.at[0], nz.at[1], a_send.at[0], a_recv.at[0], sub=left),
        remote(nst.at[1], nz.at[0], a_send.at[1], a_recv.at[1], sub=right),
        remote(lge.at[0], lez.at[1], a_send.at[2], a_recv.at[2], sub=left),
        remote(lge.at[1], lez.at[0], a_send.at[3], a_recv.at[3], sub=right),
    ]

    for k in range(FD):
        share(5 + k, 2 + k)
    chip["fe"].wait()
    fge[...] = fge[...] + fge_r[...]
    fex[b] = fge[...]
    fx = []
    for d in range(1, B):
        to = lax.rem(b + d, B)
        fx.append(
            remote(fst.at[to, pl.ds(2, FD)], fxr.at[b, pl.ds(2, FD)], x_send.at[d, 4],
                   x_recv.at[d, 4], blk=to)
        )
        fx.append(remote(fge, fex.at[b], x_send.at[d, 5], x_recv.at[d, 5], blk=to))

    for copy in cz:
        copy.wait()
    piece = csum[s // PS, lax.rem(s, PS)]
    for d in range(1, S):
        piece = piece + zr[lax.rem(s + d, S)].astype(F32)
    zg[s] = piece.astype(zg.dtype)
    cg = []
    for d in range(1, S):
        to = lax.rem(s + d, S)
        cg.append(remote(zg.at[s], zg.at[s], z_send.at[d, 2], z_recv.at[d, 2], sub=to))
    cf = [remote(zg.at[s], zg2.at[s], z_send.at[0, 0], z_recv.at[0, 0], rep=other)]
    edge_sum = cez[0]
    for d in range(1, S):
        edge_sum = edge_sum + cez[d]
    for k in range(CB):
        cge_out[k] = edge_sum[k, 0:6, :]
    loss_out[...] = edge_sum[0, 6:7, 0:128] / edge_sum[0, 7:8, 0:128]

    for copy in fx + nx:
        copy.wait()
    for k in range(FD):
        value = fown[2 + k]
        for d in range(1, B):
            value = value + fxr[lax.rem(b + d, B), 2 + k].astype(F32)
        if k == 0:
            value = value + nz[0].astype(F32)
        if k == FD - 1:
            value = value + nz[1].astype(F32)
        fg[b, k] = value.astype(BF16)
    fgc = []
    for d in range(1, B):
        to = lax.rem(b + d, B)
        fgc.append(remote(fg.at[b], fg.at[b], a_send.at[4 + d], a_recv.at[4 + d], blk=to))
    ff = [remote(fg.at[b], fg2.at[b], a_send.at[4], a_recv.at[4], rep=other)]
    edge_sum = fex[0]
    for d in range(1, B):
        edge_sum = edge_sum + fex[d]
    for k in range(FD):
        value = edge_sum[k]
        if k == 0:
            value = value + lez[0]
        if k == FD - 1:
            value = value + lez[1]
        fge_out[k] = value[0:6, :]

    for d in range(1, B):
        fgc[d - 1].wait()
        src = lax.rem(b + B - d, B)
        ff.append(
            remote(fg.at[src], fg2.at[src], a_send.at[4 + B - 1 + d], a_recv.at[4 + B - 1 + d],
                   rep=other)
        )
    for d in range(1, S):
        cg[d - 1].wait()
        src = lax.rem(s + S - d, S)
        cf.append(
            remote(zg.at[src], zg2.at[src], z_send.at[d, 3], z_recv.at[d, 3], rep=other)
        )
    for q in range(B):
        for k in range(FD):
            fgh_out[k, r, q] = fg[q, k].astype(F32)
    for p in range(S):
        cgh_out[p // PS, r, p % PS] = zg[p].astype(F32)
    for copy in ff:
        copy.wait()
    for q in range(B):
        for k in range(FD):
            fgh_out[k, other, q] = fg2[q, k].astype(F32)
    for copy in cf:
        copy.wait()
    for p in range(S):
        cgh_out[p // PS, other, p % PS] = zg2[p].astype(F32)


def shards(points, source, speed, live_count, index, fine_hidden, fine_edge, coarse_hidden,
           coarse_edge):
    S, B = lax.axis_size("sub"), lax.axis_size("blk")
    NP = points.shape[1]
    FD, H = fine_hidden.shape[0], fine_hidden.shape[1]
    CB = coarse_hidden.shape[0]
    C = CB * B
    PS = S // CB
    cap = index.shape[1]
    half = H // 2
    Q = half // B
    RP = half // PS
    wire = BF16 if RP % 16 == 0 else F32
    NE = FD + 5
    vm, dma = pltpu.VMEM, pltpu.SemaphoreType.DMA
    scratch = [
        vm((C, H, H), BF16), vm((C, 8, H), F32), vm((FD, 8, H), F32),
        vm((H, H), BF16), vm((H, H), BF16), vm((8, H), F32), vm((8, H), F32),
        vm((128, NP), F32), vm((NP, 128), F32), vm((128, 128), F32), vm((128, 128), F32),
        vm((NP, 128), F32), vm((128, NP), F32),
        vm((NP, 128), F32), vm((128, 128), F32), vm((NP, 128), F32), vm((128, 128), F32),
        vm((8, 128), jnp.int32),
        vm((FD + 3, 7, NP, H), BF16), vm((FD + 3, 7, NP, H), F32), vm((FD + 3, NP, H), F32),
        vm((2, 7, cap, H), BF16), vm((2, 7, cap, H), F32), vm((2, cap, H), F32),
        vm((7, NP, H), BF16),
        vm((NE, 2, B, Q, H), F32), vm((NE, B, Q, H), F32),
        vm((C, 8, H), F32), vm((C, 8, H), F32), vm((2, 8, H), F32), vm((2, 8, H), F32),
        vm((FD, 8, H), F32), vm((FD, 8, H), F32),
        vm((C, PS, RP, H), F32), vm((C, PS, RP, H), wire), vm((B, CB, PS, RP, H), wire),
        vm((CB, PS, RP, H), F32), vm((CB, PS, RP, H), wire), vm((S, RP, H), wire),
        vm((S, RP, H), wire), vm((S, RP, H), wire), vm((B, CB, 8, H), F32),
        vm((S, CB, 8, H), F32),
        vm((2 + FD, Q, H), F32), vm((B, 2 + FD, Q, H), BF16), vm((B, 2 + FD, Q, H), BF16),
        vm((2, Q, H), BF16), vm((2, Q, H), BF16), vm((B, 2, 8, H), F32), vm((2, 8, H), F32),
        vm((B, FD, 8, H), F32),
        vm((8, 128), F32), vm((B, FD, Q, H), BF16), vm((B, FD, Q, H), BF16),
        dma((4 + 2 * B,)), dma((4 + 2 * B,)), dma((NE + 3,)), dma((NE + 3,)),
        dma((B, 6)), dma((B, 6)), dma((S, 4)), dma((S, 4)),
        dma((4 + 2 * B,)), dma((4 + 2 * B,)),
    ]
    space = pl.BlockSpec(memory_space=pltpu.VMEM)
    outs = pl.pallas_call(
        functools.partial(kernel, S, B, CB, FD),
        out_shape=(
            jax.ShapeDtypeStruct((1, NP), F32),
            jax.ShapeDtypeStruct((FD, 2, B, Q, H), F32),
            jax.ShapeDtypeStruct((FD, 6, H), F32),
            jax.ShapeDtypeStruct((CB, 2, PS, RP, H), F32),
            jax.ShapeDtypeStruct((CB, 6, H), F32),
            jax.ShapeDtypeStruct((1, 128), F32),
        ),
        in_specs=[space] * 3 + [pl.BlockSpec(memory_space=pltpu.SMEM)] + [space] * 5,
        out_specs=(space,) * 6,
        scratch_shapes=scratch,
        compiler_params=pltpu.CompilerParams(
            collective_id=0, has_side_effects=True, vmem_limit_bytes=56 * 1024 * 1024
        ),
    )(
        points, source.reshape(1, NP), speed.reshape(1, NP), live_count, index,
        fine_hidden, fine_edge, coarse_hidden, coarse_edge,
    )
    return (
        outs[0].reshape(NP), outs[1].reshape(FD, H, H), outs[2], outs[3].reshape(CB, H, H),
        outs[4], outs[5][0, 0:1],
    )


def solution(mesh):
    return jax.shard_map(
        shards,
        mesh=mesh,
        in_specs=(
            P(None, ("groups", "sub", "blk", "rep")),
            P(("groups", "sub", "blk", "rep")),
            P(("groups", "sub", "blk", "rep")),
            P(("groups", "sub", "blk", "rep")),
            P(None, ("groups", "sub", "blk", "rep")),
            P("sub", None, None),
            P("sub", None, None),
            P("blk", None, None),
            P("blk", None, None),
        ),
        out_specs=(
            P(("groups", "sub", "blk", "rep")),
            P(("groups", "sub"), None, None),
            P(("groups", "sub"), None, None),
            P(("groups", "blk"), None, None),
            P(("groups", "blk"), None, None),
            P("groups"),
        ),
        check_vma=False,
    )
```

```python
import functools

import jax
import jax.numpy as jnp
from jax import lax
from jax.experimental import pallas as pl
from jax.experimental.pallas import tpu as pltpu
from jax.sharding import PartitionSpec as P

MESH = pl.DeviceIdType.MESH
F32 = jnp.float32
BF16 = jnp.bfloat16
WIDTH_SQ = 0.36
CHUNK = 16
UNROLL = 8
EXACT = lax.Precision.HIGHEST


def wide(tile, columns):
    return jnp.concatenate([tile] * (columns // tile.shape[1]), axis=1)


def fold(value):
    total = value[0:8]
    for at in range(8, value.shape[0], 8):
        total = total + value[at : at + 8]
    return total


def rows_of(step):
    return pl.ds(pl.multiple_of(step * CHUNK, CHUNK), CHUNK)


def window_rows(dx, width_sq, speed):
    weight = jnp.exp(-dx * dx / width_sq)
    weight_x = -2.0 * dx / width_sq * weight
    weight_xx = (4.0 * dx * dx / (width_sq * width_sq) - 2.0 / width_sq) * weight
    return (weight, speed * weight, 2.0 * speed * weight_x, speed * weight_xx)


class Net:
    def __init__(self, count, factors, edge, weights, cols, offset, ids, streams, layers, hidden):
        self.count, self.factors = count, factors
        self.edge, self.weights = edge, weights
        self.cols, self.offset, self.ids = cols, offset, ids
        self.streams, self.layers, self.hidden = streams, layers, hidden

    def col(self, name, step):
        at = self.ids[name]
        rows = pl.ds(pl.multiple_of(self.offset + step * CHUNK, CHUNK), CHUNK)
        return self.cols[rows, at : at + 1]

    def forward(self, totals):
        edge = self.edge()
        e = [edge[j : j + 1] for j in range(6)]
        columns = edge.shape[1]
        scaled = [self.factors[d] * e[d] for d in range(3)]
        squares = [s * s for s in scaled]

        def first(step, carry):
            rows = rows_of(step)
            pre = (
                self.col("t", step) * e[0]
                + self.col("x", step) * e[1]
                + self.col("y", step) * e[2]
                + e[3]
            )
            h = jnp.tanh(pre)
            g = 1.0 - h * h
            s = -2.0 * h * g
            self.hidden[rows, :] = h
            self.streams[0, rows, :] = h.astype(BF16)
            for d in range(3):
                self.streams[1 + d, rows, :] = (g * scaled[d]).astype(BF16)
                self.streams[4 + d, rows, :] = (s * squares[d]).astype(BF16)
            return carry

        steps = self.count // CHUNK
        lax.fori_loop(0, steps, first, 0, unroll=UNROLL)
        flat = self.streams[...].reshape(7 * self.count, columns)
        self.layers[...] = jnp.dot(
            flat, self.weights(), preferred_element_type=F32
        ).reshape(7, self.count, columns)
        out = e[5] * (1.0 / float(columns) ** 0.5)

        def second(step, carry):
            rows = rows_of(step)
            w, cw = self.col("w", step), self.col("cw", step)
            cx, cxx = self.col("cx", step), self.col("cxx", step)
            k = jnp.tanh(self.layers[0, rows, :] + e[4])
            m = 1.0 - k * k
            l1, l2, l3 = [self.layers[j, rows, :] for j in (1, 2, 3)]
            curved = (
                w * self.layers[4, rows, :]
                - cw * (self.layers[5, rows, :] + self.layers[6, rows, :])
                - cx * l2
            )
            q = w * (l1 * l1) - cw * (l2 * l2 + l3 * l3)
            v = curved - 2.0 * k * q
            t = m * v - cxx * k
            self.layers[0, rows, :] = k
            self.layers[4, rows, :] = v
            self.layers[5, rows, :] = q
            self.layers[6, rows, :] = t
            value = jnp.sum(t * out, axis=1, keepdims=True)
            at = pl.ds(pl.multiple_of(self.offset + step * CHUNK, CHUNK), CHUNK)
            totals[at, :] = totals[at, :] + jnp.broadcast_to(value, (CHUNK, 128))
            return carry

        lax.fori_loop(0, steps, second, 0, unroll=UNROLL)

    def backward(self, cotangent, grads, grad_out, edge_out):
        edge = self.edge()
        e = [edge[j : j + 1] for j in range(6)]
        columns = edge.shape[1]
        norm = 1.0 / float(columns) ** 0.5
        out = e[5] * norm
        scaled = [self.factors[d] * e[d] for d in range(3)]
        squares = [s * s for s in scaled]
        zero = jnp.zeros((8, columns), F32)
        steps = self.count // CHUNK
        low = grads.at[:, pl.ds(0, self.count), :]

        def first(step, carry):
            rows = rows_of(step)
            at = pl.ds(pl.multiple_of(self.offset + step * CHUNK, CHUNK), CHUNK)
            cot = wide(cotangent[at, :], columns)
            w, cw = self.col("w", step), self.col("cw", step)
            cx, cxx = self.col("cx", step), self.col("cxx", step)
            k, l1, l2, l3, v, q, t = [self.layers[j, rows, :] for j in range(7)]
            m = 1.0 - k * k
            com = cot * out * m
            k4 = 4.0 * k * com
            kc = k4 * cw
            g0 = com * (-2.0 * (k * v + m * q) - cxx)
            low[0, rows, :] = g0.astype(BF16)
            low[1, rows, :] = (-(k4 * w) * l1).astype(BF16)
            low[2, rows, :] = (kc * l2 - com * cx).astype(BF16)
            low[3, rows, :] = (kc * l3).astype(BF16)
            low[4, rows, :] = (com * w).astype(BF16)
            minus = (-(com * cw)).astype(BF16)
            low[5, rows, :] = minus
            low[6, rows, :] = minus
            return (carry[0] + fold(g0), carry[1] + fold(cot * t))

        sum4, sum5 = lax.fori_loop(0, steps, first, (zero, zero), unroll=UNROLL)
        flat = self.streams[...].reshape(7 * self.count, columns)
        flat_low = low[...].reshape(7 * self.count, columns)
        grad_out(
            lax.dot_general(
                flat, flat_low, (((0,), (0,)), ((), ())), preferred_element_type=F32
            )
        )
        self.layers[...] = lax.dot_general(
            flat_low, self.weights(), (((1,), (1,)), ((), ())), preferred_element_type=F32
        ).reshape(7, self.count, columns)

        def second(step, carry):
            rows = rows_of(step)
            h = self.hidden[rows, :]
            i = [self.layers[j, rows, :] for j in range(7)]
            h2 = h * h
            g = 1.0 - h2
            s = -2.0 * h * g
            lin = i[1] * scaled[0] + i[2] * scaled[1] + i[3] * scaled[2]
            quad = i[4] * squares[0] + i[5] * squares[1] + i[6] * squares[2]
            da = g * (i[0] - 2.0 * h * lin + (6.0 * h2 - 2.0) * quad)
            terms = [
                da,
                da * self.col("t", step),
                da * self.col("x", step),
                da * self.col("y", step),
            ]
            terms += [g * i[1 + d] for d in range(3)] + [s * i[4 + d] for d in range(3)]
            return tuple(c + fold(x) for c, x in zip(carry, terms))

        sums = lax.fori_loop(0, steps, second, (zero,) * 10, unroll=UNROLL)
        sums = [jnp.sum(x, axis=0, keepdims=True) for x in sums]
        rows = [
            sums[1 + d]
            + self.factors[d] * sums[4 + d]
            + 2.0 * self.factors[d] * scaled[d] * sums[7 + d]
            for d in range(3)
        ]
        rows.append(sums[0])
        rows.append(jnp.sum(sum4, axis=0, keepdims=True))
        rows.append(jnp.sum(sum5, axis=0, keepdims=True) * norm)
        for j, row in enumerate(rows):
            edge_out(j, row)


def row_tile(tile):
    return tile.T[0:8, :]


def column_tile(row):
    return jnp.broadcast_to(row, (row.shape[1], row.shape[1])).T


def kernel(
    S, B, CB, FD, points_ref, source_ref, speed_ref, live_ref, index_ref, fh_ref, fe_ref, ch_ref,
    ce_ref, res_out, fg, fge_out, zg, cge_out,
    cedge, fedge, rows_sc, cols, idx_sc, pick_t, pts, lsend, lrecv,
    totals, ltotals, cback, crecv, lback, lcr, cotr, cotc, lcots, lcotr, lcotc,
    st, layers, hid, stl, ll, hl, grads, gh, gr, cge, cge_r, fge, fge_r,
    csum, zst, zr, cez, fown, fst, fxr, fex,
    p_send, p_recv, chip_send, chip_recv, x_send, x_recv, z_send, z_recv, g_send, g_recv,
):
    C = CB * B
    PS = S // CB
    NP = points_ref.shape[1]
    cap = index_ref.shape[1]
    H = fh_ref.shape[1]
    s, b, r = lax.axis_index("sub"), lax.axis_index("blk"), lax.axis_index("rep")
    other = 1 - r
    right, left = lax.rem(s + 1, S), lax.rem(s + S - 1, S)
    peers = [lax.rem(b + d, B) for d in range(1, B)]
    cell = s // max(S // C, 1)
    half_width = float(FD * S) / float(C)
    start = s.astype(F32) * FD

    barrier = pltpu.get_barrier_semaphore()
    pl.semaphore_signal(barrier, inc=1, device_id={"rep": other}, device_id_type=MESH)
    for to in peers:
        pl.semaphore_signal(barrier, inc=1, device_id={"blk": to}, device_id_type=MESH)
    for d in range(1, S):
        pl.semaphore_signal(
            barrier, inc=1, device_id={"sub": lax.rem(s + d, S)}, device_id_type=MESH
        )

    fields = jnp.concatenate(
        [points_ref[...], speed_ref[...], jnp.zeros((4, NP), F32)], axis=0
    )
    pts[b] = fields
    x_rows = lax.broadcasted_iota(jnp.int32, (8, 128), 0) == 1
    idx_sc[...] = jnp.full_like(idx_sc, -1)
    for n in range(2):
        idx_sc[n : n + 1, 0:cap] = index_ref[n : n + 1, :]
        pick_t[n] = (
            lax.broadcasted_iota(jnp.int32, (NP, 128), 0) == idx_sc[n : n + 1, :]
        ).astype(F32)
        listed = jnp.dot(fields, pick_t[n], preferred_element_type=F32, precision=EXACT)
        centre = start - 0.5 if n == 0 else start + (FD + 0.5)
        lsend[n] = listed - jnp.where(x_rows, centre, 0.0)
    pl.semaphore_wait(barrier, S + B - 1)

    def remote(src, dst, send, recv, **where):
        copy = pltpu.make_async_remote_copy(
            src_ref=src, dst_ref=dst, send_sem=send, recv_sem=recv,
            device_id=where, device_id_type=MESH,
        )
        copy.start()
        return copy

    def to_sides(src, dst, at):
        return [
            remote(src.at[0], dst.at[1], p_send.at[at], p_recv.at[at], sub=left),
            remote(src.at[1], dst.at[0], p_send.at[at + 1], p_recv.at[at + 1], sub=right),
        ]

    def to_peers(src_at, dst, at):
        return [
            remote(src_at(to), dst.at[b], p_send.at[at + d], p_recv.at[at + d], blk=to)
            for d, to in enumerate(peers)
        ]

    lists_in = to_sides(lsend, lrecv, 0)
    points_in = to_peers(lambda to: pts.at[b], pts, 6)

    fine_edges = fe_ref[...].astype(F32)
    coarse_edges = ce_ref[...].astype(F32)
    for j in range(6):
        for k in range(FD):
            fedge[k, j : j + 1, :] = fine_edges[j][k : k + 1]
        for k in range(CB):
            cedge[k, j : j + 1, :] = coarse_edges[j][k : k + 1]

    fine_f = (2.0, 2.0, 2.0)
    coarse_f = (2.0, 2.0 / half_width, 2.0)

    def put(at, group):
        for j, row in enumerate(group):
            rows_sc[at + j : at + j + 1, :] = row
        return {"t": 0, "y": 1, "x": at, "w": at + 1, "cw": at + 2, "cx": at + 3, "cxx": at + 4}

    def time_and_y(block):
        rows_sc[0:1, :] = 2.0 * (block[0:1] - 0.5)
        rows_sc[1:2, :] = 2.0 * (block[2:3] - 0.5)

    def fine_rows(at, block, centre):
        dx = block[1:2] - centre
        return put(at, [2.0 * dx, *window_rows(dx, WIDTH_SQ, block[3:4])])

    def coarse_rows(at, block, k):
        shift = lax.rem(b * CB + k - cell + 1 + C, C)
        used = jnp.where(shift < 3, 1.0, 0.0).astype(F32)
        dx = block[1:2] - (cell.astype(F32) + (shift.astype(F32) - 0.5)) * half_width
        window = window_rows(dx, WIDTH_SQ * half_width * half_width, block[3:4])
        return put(at, [2.0 * dx / half_width, *(used * row for row in window)])

    rows_sc[...] = jnp.zeros_like(rows_sc)
    totals[...] = jnp.zeros_like(totals)
    ltotals[...] = jnp.zeros_like(ltotals)

    def coarse_net(place, k, ids):
        at = FD + place * CB + k
        return Net(NP, coarse_f, lambda: cedge[k], lambda: ch_ref[k], cols.at[place], 0, ids,
                   st.at[at], layers.at[at], hid.at[at])

    time_and_y(fields)
    fine_ids = [fine_rows(2 + 5 * k, fields, start + (k + 0.5)) for k in range(FD)]
    coarse_ids = [coarse_rows(2 + 5 * (FD + k), fields, k) for k in range(CB)]
    cols[0] = rows_sc[...].T
    fine = [
        Net(NP, fine_f, lambda k=k: fedge[k], lambda k=k: fh_ref[k], cols.at[0], 0,
            fine_ids[k], st.at[k], layers.at[k], hid.at[k])
        for k in range(FD)
    ]
    coarse = [[coarse_net(0, k, coarse_ids[k]) for k in range(CB)]]
    for net in fine:
        net.forward(totals.at[0])

    for copy in points_in:
        copy.wait()
    for d, source in enumerate(peers):
        block = pts[source]
        time_and_y(block)
        ids = [coarse_rows(2 + 5 * k, block, k) for k in range(CB)]
        cols[1 + d] = rows_sc[...].T
        nets = [coarse_net(1 + d, k, ids[k]) for k in range(CB)]
        coarse.append(nets)
        for net in nets:
            net.forward(totals.at[1 + d])
        cback[source] = row_tile(totals[1 + d])
    coarse_back = to_peers(lambda to: cback.at[to], crecv, 6 + B)

    for copy in lists_in:
        copy.wait()
    lists = []
    for n, k in ((0, 0), (1, FD - 1)):
        block = lrecv[n]
        time_and_y(block)
        ids = fine_rows(2, block, 0.0)
        cols[B + n] = rows_sc[...].T
        net = Net(cap, fine_f, lambda k=k: fedge[k], lambda k=k: fh_ref[k], cols.at[B + n], 0,
                  ids, stl.at[n], ll.at[n], hl.at[n])
        lists.append(net)
        net.forward(ltotals.at[n])
        lback[n] = row_tile(ltotals[n])
    lists_back = to_sides(lback, lcr, 2)

    for net in coarse[0]:
        net.forward(totals.at[0])
    total = row_tile(totals[0])
    for copy in coarse_back + lists_back:
        copy.wait()
    for source in peers:
        total = total + crecv[source]
    for n in range(2):
        total = total + lax.dot_general(
            lcr[n], pick_t[n], (((1,), (1,)), ((), ())), preferred_element_type=F32,
            precision=EXACT,
        )
    count = live_ref[0]
    live = (lax.broadcasted_iota(jnp.int32, (1, NP), 1) < count).astype(F32)
    residual = (total[0:1] * 0.125 - source_ref[...]) * live
    res_out[...] = residual
    cot = residual * 0.125
    loss = jnp.broadcast_to(jnp.sum(residual * residual, axis=1, keepdims=True), (1, NP))
    counted = jnp.full((1, NP), 1.0, F32) * count.astype(F32)
    cotr[b] = jnp.concatenate([cot, loss, counted, jnp.zeros((5, NP), F32)], axis=0)
    cot8 = jnp.broadcast_to(cot, (8, NP))
    for n in range(2):
        lcots[n] = jnp.dot(cot8, pick_t[n], preferred_element_type=F32, precision=EXACT)
    lists_cot = to_sides(lcots, lcotr, 4)
    peers_cot = to_peers(lambda to: cotr.at[b], cotr, 6 + 2 * B)
    cotc[0] = column_tile(cot)
    cge[...] = jnp.zeros_like(cge)
    fge[...] = jnp.zeros_like(fge)

    def run_back(e, net, cotangent, edge_ref, k, more):
        def keep(value):
            value = value.reshape(gh.shape[1:])
            gh[e] = gh[e] + value if more else value

        def keep_edge(j, row):
            edge_ref[k, j : j + 1, :] = edge_ref[k, j : j + 1, :] + row

        net.backward(cotangent, grads, keep, keep_edge)

    def to_core(e):
        return remote(gh.at[e, other], gr.at[e], chip_send.at[e], chip_recv.at[e], rep=other)

    NE = CB + FD
    chip = {}
    for k in range(CB):
        run_back(k, coarse[0][k], cotc.at[0], cge, k, False)
    for copy in peers_cot:
        copy.wait()
    for d, source in enumerate(peers):
        cotc[1 + d] = column_tile(cotr[source, 0:1, :])
    for k in range(CB):
        for d in range(B - 1):
            run_back(k, coarse[1 + d][k], cotc.at[1 + d], cge, k, True)
        chip[k] = to_core(k)
    sums = cotr[0]
    for q in range(1, B):
        sums = sums + cotr[q]
    cge[0, 6:8, :] = wide(sums[1:3], H)
    chip["ce"] = remote(cge, cge_r, chip_send.at[NE], chip_recv.at[NE], rep=other)

    run_back(CB, fine[0], cotc.at[0], fge, 0, False)

    cz = []
    for k in range(CB):
        chip[k].wait()
        value = (gh[k, r] + gr[k]).reshape(csum.shape[1:])
        csum[k] = value
        zst[k] = value.astype(zst.dtype)
    for d in range(1, S):
        to = lax.rem(s + d, S)
        cz.append(
            remote(zst.at[to // PS, lax.rem(to, PS)], zr.at[s], z_send.at[d, 0],
                   z_recv.at[d, 0], sub=to)
        )
    chip["ce"].wait()
    cez[s] = cge[...] + cge_r[...]
    for d in range(1, S):
        to = lax.rem(s + d, S)
        cz.append(remote(cez.at[s], cez.at[s], z_send.at[d, 1], z_recv.at[d, 1], sub=to))

    for k in range(1, FD):
        run_back(CB + k, fine[k], cotc.at[0], fge, k, False)
    for copy in lists_cot:
        copy.wait()
    for n, k in ((0, 0), (1, FD - 1)):
        lcotc[n] = column_tile(lcotr[n, 0:1, :])
        run_back(CB + k, lists[n], lcotc.at[n], fge, k, True)
    for k in range(FD):
        chip[CB + k] = to_core(CB + k)
    chip["fe"] = remote(fge, fge_r, chip_send.at[NE + 1], chip_recv.at[NE + 1], rep=other)

    fx = []
    for k in range(FD):
        chip[CB + k].wait()
        fown[k] = gh[CB + k, r, b] + gr[CB + k, b]
        for d, to in enumerate(peers):
            fst[to, k] = (gh[CB + k, r, to] + gr[CB + k, to]).astype(BF16)
    for d, to in enumerate(peers):
        fx.append(remote(fst.at[to], fxr.at[b], x_send.at[d, 0], x_recv.at[d, 0], blk=to))
    chip["fe"].wait()
    fex[b] = fge[...] + fge_r[...]
    for d, to in enumerate(peers):
        fx.append(remote(fex.at[b], fex.at[b], x_send.at[d, 1], x_recv.at[d, 1], blk=to))

    for copy in cz:
        copy.wait()
    piece = csum[s // PS, lax.rem(s, PS)]
    for d in range(1, S):
        piece = piece + zr[lax.rem(s + d, S)].astype(F32)
    zg[r, s] = piece.astype(zg.dtype)
    cg = []
    for d in range(1, S):
        to = lax.rem(s + d, S)
        cg.append(remote(zg.at[r, s], zg.at[r, s], z_send.at[d, 2], z_recv.at[d, 2], sub=to))
    last = [remote(zg.at[r, s], zg.at[r, s], z_send.at[0, 0], z_recv.at[0, 0], rep=other)]
    edge_sum = cez[0]
    for d in range(1, S):
        edge_sum = edge_sum + cez[d]
    cge_out[...] = edge_sum

    for copy in fx:
        copy.wait()
    for k in range(FD):
        value = fown[k]
        for source in peers:
            value = value + fxr[source, k].astype(F32)
        fg[r, b, k] = value.astype(BF16)
    fgc = [
        remote(fg.at[r, b], fg.at[r, b], g_send.at[1 + d], g_recv.at[1 + d], blk=to)
        for d, to in enumerate(peers)
    ]
    last.append(remote(fg.at[r, b], fg.at[r, b], g_send.at[0], g_recv.at[0], rep=other))
    edge_sum = fex[0]
    for q in range(1, B):
        edge_sum = edge_sum + fex[q]
    fge_out[...] = edge_sum

    for d in range(B - 1):
        fgc[d].wait()
        source = lax.rem(b + B - 1 - d, B)
        last.append(
            remote(fg.at[r, source], fg.at[r, source], g_send.at[B + d], g_recv.at[B + d],
                   rep=other)
        )
    for d in range(1, S):
        cg[d - 1].wait()
        source = lax.rem(s + S - d, S)
        last.append(
            remote(zg.at[r, source], zg.at[r, source], z_send.at[d, 3], z_recv.at[d, 3],
                   rep=other)
        )
    for copy in last:
        copy.wait()


def finish(res_in, fg, fe, zg, ce, res_out, fgh_out, fge_out, cgh_out, cge_out, loss_out):
    B, FD = fg.shape[1], fg.shape[2]
    S, CB = zg.shape[1], ce.shape[0]
    PS = S // CB
    res_out[...] = res_in[...]
    for half in range(2):
        for q in range(B):
            for k in range(FD):
                fgh_out[k, half, q] = fg[half, q, k].astype(F32)
        for p in range(S):
            cgh_out[p // PS, half, p % PS] = zg[half, p].astype(F32)
    for j in range(6):
        for k in range(FD):
            fge_out[j, k : k + 1, :] = fe[k, j : j + 1, :]
        for k in range(CB):
            cge_out[j, k : k + 1, :] = ce[k, j : j + 1, :]
    loss = ce[0, 6:7, 0:128] / ce[0, 7:8, 0:128]
    loss_out[0] = loss[0, 0]


def shards(points, source, speed, live_count, index, fine_hidden, fine_edge, coarse_hidden,
           coarse_edge):
    S, B = lax.axis_size("sub"), lax.axis_size("blk")
    NP = points.shape[1]
    FD, H = fine_hidden.shape[0], fine_hidden.shape[1]
    CB = coarse_hidden.shape[0]
    PS = S // CB
    cap = index.shape[1]
    half = H // 2
    Q = half // B
    RP = half // PS
    wire = BF16 if RP % 16 == 0 else F32
    NE = FD + CB
    NN = FD + B * CB
    vm, dma = pltpu.VMEM, pltpu.SemaphoreType.DMA
    scratch = [
        vm((CB, 8, H), F32), vm((FD, 8, H), F32), vm((128, NP), F32), vm((B + 2, NP, 128), F32),
        vm((8, 128), jnp.int32), vm((2, NP, 128), F32), vm((B, 8, NP), F32),
        vm((2, 8, 128), F32), vm((2, 8, 128), F32),
        vm((B, NP, 128), F32), vm((2, NP, 128), F32), vm((B, 8, NP), F32), vm((B, 8, NP), F32),
        vm((2, 8, NP), F32), vm((2, 8, NP), F32), vm((B, 8, NP), F32), vm((B, NP, 128), F32),
        vm((2, 8, 128), F32), vm((2, 8, 128), F32), vm((2, NP, 128), F32),
        vm((NN, 7, NP, H), BF16), vm((NN, 7, NP, H), F32), vm((NN, NP, H), F32),
        vm((2, 7, cap, H), BF16), vm((2, 7, cap, H), F32), vm((2, cap, H), F32),
        vm((7, NP, H), BF16),
        vm((NE, 2, B, Q, H), F32), vm((NE, B, Q, H), F32),
        vm((CB, 8, H), F32), vm((CB, 8, H), F32), vm((FD, 8, H), F32), vm((FD, 8, H), F32),
        vm((CB, PS, RP, H), F32), vm((CB, PS, RP, H), wire), vm((S, RP, H), wire),
        vm((S, CB, 8, H), F32),
        vm((FD, Q, H), F32), vm((B, FD, Q, H), BF16), vm((B, FD, Q, H), BF16),
        vm((B, FD, 8, H), F32),
        dma((6 + 3 * B,)), dma((6 + 3 * B,)), dma((NE + 2,)), dma((NE + 2,)),
        dma((B, 2)), dma((B, 2)), dma((S, 4)), dma((S, 4)), dma((2 * B,)), dma((2 * B,)),
    ]
    space = pl.BlockSpec(memory_space=pltpu.VMEM)
    scalar = pl.BlockSpec(memory_space=pltpu.SMEM)
    shape = jax.ShapeDtypeStruct
    parts = pl.pallas_call(
        functools.partial(kernel, S, B, CB, FD),
        out_shape=(
            shape((1, NP), F32),
            shape((2, B, FD, Q, H), BF16),
            shape((FD, 8, H), F32),
            shape((2, S, RP, H), wire),
            shape((CB, 8, H), F32),
        ),
        in_specs=[space] * 3 + [scalar] + [space] * 5,
        out_specs=(space,) * 5,
        scratch_shapes=scratch,
        compiler_params=pltpu.CompilerParams(
            collective_id=0, has_side_effects=True, vmem_limit_bytes=56 * 1024 * 1024
        ),
    )(
        points, source.reshape(1, NP), speed.reshape(1, NP), live_count, index,
        fine_hidden, fine_edge.transpose(1, 0, 2), coarse_hidden, coarse_edge.transpose(1, 0, 2),
    )
    outs = pl.pallas_call(
        finish,
        out_shape=(
            shape((1, NP), F32),
            shape((FD, 2, B, Q, H), F32),
            shape((6, FD, H), F32),
            shape((CB, 2, PS, RP, H), F32),
            shape((6, CB, H), F32),
            shape((1,), F32),
        ),
        in_specs=[space] * 5,
        out_specs=(space,) * 5 + (scalar,),
        compiler_params=pltpu.CompilerParams(vmem_limit_bytes=32 * 1024 * 1024),
    )(*parts)
    return (
        outs[0].reshape(NP), outs[1].reshape(FD, H, H), outs[2].transpose(1, 0, 2),
        outs[3].reshape(CB, H, H), outs[4].transpose(1, 0, 2), outs[5],
    )


def solution(mesh):
    return jax.shard_map(
        shards,
        mesh=mesh,
        in_specs=(
            P(None, ("groups", "sub", "blk", "rep")),
            P(("groups", "sub", "blk", "rep")),
            P(("groups", "sub", "blk", "rep")),
            P(("groups", "sub", "blk", "rep")),
            P(None, ("groups", "sub", "blk", "rep")),
            P("sub", None, None),
            P("sub", None, None),
            P("blk", None, None),
            P("blk", None, None),
        ),
        out_specs=(
            P(("groups", "sub", "blk", "rep")),
            P(("groups", "sub"), None, None),
            P(("groups", "sub"), None, None),
            P(("groups", "blk"), None, None),
            P(("groups", "blk"), None, None),
            P("groups"),
        ),
        check_vma=False,
    )
```

```python
import functools

import jax
import jax.numpy as jnp
from jax import lax
from jax.experimental import pallas as pl
from jax.experimental.pallas import tpu as pltpu
from jax.sharding import PartitionSpec as P

MESH = pl.DeviceIdType.MESH
F32 = jnp.float32
BF16 = jnp.bfloat16
WIDTH_SQ = 0.36
CHUNK = 16
UNROLL = 8
EXACT = lax.Precision.HIGHEST


def wide(tile, columns):
    return jnp.concatenate([tile] * (columns // tile.shape[1]), axis=1)


def fold(value):
    total = value[0:8]
    for at in range(8, value.shape[0], 8):
        total = total + value[at : at + 8]
    return total


def rows_of(step):
    return pl.ds(pl.multiple_of(step * CHUNK, CHUNK), CHUNK)


def window_rows(dx, width_sq, speed):
    weight = jnp.exp(-dx * dx / width_sq)
    weight_x = -2.0 * dx / width_sq * weight
    weight_xx = (4.0 * dx * dx / (width_sq * width_sq) - 2.0 / width_sq) * weight
    return (weight, speed * weight, 2.0 * speed * weight_x, speed * weight_xx)


class Net:
    def __init__(self, count, factors, edge, weights, cols, offset, ids, streams, layers, hidden):
        self.count, self.factors = count, factors
        self.edge, self.weights = edge, weights
        self.cols, self.offset, self.ids = cols, offset, ids
        self.streams, self.layers, self.hidden = streams, layers, hidden

    def col(self, name, step):
        at = self.ids[name]
        rows = pl.ds(pl.multiple_of(self.offset + step * CHUNK, CHUNK), CHUNK)
        return self.cols[rows, at : at + 1]

    def forward(self, totals):
        edge = self.edge()
        e = [edge[j : j + 1] for j in range(6)]
        columns = edge.shape[1]
        scaled = [self.factors[d] * e[d] for d in range(3)]
        squares = [s * s for s in scaled]

        def first(step, carry):
            rows = rows_of(step)
            pre = (
                self.col("t", step) * e[0]
                + self.col("x", step) * e[1]
                + self.col("y", step) * e[2]
                + e[3]
            )
            h = jnp.tanh(pre)
            g = 1.0 - h * h
            s = -2.0 * h * g
            self.hidden[rows, :] = h
            self.streams[0, rows, :] = h.astype(BF16)
            for d in range(3):
                self.streams[1 + d, rows, :] = (g * scaled[d]).astype(BF16)
                self.streams[4 + d, rows, :] = (s * squares[d]).astype(BF16)
            return carry

        steps = self.count // CHUNK
        lax.fori_loop(0, steps, first, 0, unroll=UNROLL)
        flat = self.streams[...].reshape(7 * self.count, columns)
        self.layers[...] = jnp.dot(
            flat, self.weights(), preferred_element_type=F32
        ).reshape(7, self.count, columns)
        out = e[5] * (1.0 / float(columns) ** 0.5)

        def second(step, carry):
            rows = rows_of(step)
            w, cw = self.col("w", step), self.col("cw", step)
            cx, cxx = self.col("cx", step), self.col("cxx", step)
            k = jnp.tanh(self.layers[0, rows, :] + e[4])
            m = 1.0 - k * k
            l1, l2, l3 = [self.layers[j, rows, :] for j in (1, 2, 3)]
            curved = (
                w * self.layers[4, rows, :]
                - cw * (self.layers[5, rows, :] + self.layers[6, rows, :])
                - cx * l2
            )
            q = w * (l1 * l1) - cw * (l2 * l2 + l3 * l3)
            v = curved - 2.0 * k * q
            t = m * v - cxx * k
            self.layers[0, rows, :] = k
            self.layers[4, rows, :] = v
            self.layers[5, rows, :] = q
            self.layers[6, rows, :] = t
            value = jnp.sum(t * out, axis=1, keepdims=True)
            at = pl.ds(pl.multiple_of(self.offset + step * CHUNK, CHUNK), CHUNK)
            totals[at, :] = totals[at, :] + jnp.broadcast_to(value, (CHUNK, 128))
            return carry

        lax.fori_loop(0, steps, second, 0, unroll=UNROLL)

    def backward(self, cotangent, grads, grad_out, edge_out):
        edge = self.edge()
        e = [edge[j : j + 1] for j in range(6)]
        columns = edge.shape[1]
        norm = 1.0 / float(columns) ** 0.5
        out = e[5] * norm
        scaled = [self.factors[d] * e[d] for d in range(3)]
        squares = [s * s for s in scaled]
        zero = jnp.zeros((8, columns), F32)
        steps = self.count // CHUNK
        low = grads.at[:, pl.ds(0, self.count), :]

        def first(step, carry):
            rows = rows_of(step)
            at = pl.ds(pl.multiple_of(self.offset + step * CHUNK, CHUNK), CHUNK)
            cot = wide(cotangent[at, :], columns)
            w, cw = self.col("w", step), self.col("cw", step)
            cx, cxx = self.col("cx", step), self.col("cxx", step)
            k, l1, l2, l3, v, q, t = [self.layers[j, rows, :] for j in range(7)]
            m = 1.0 - k * k
            com = cot * out * m
            k4 = 4.0 * k * com
            kc = k4 * cw
            g0 = com * (-2.0 * (k * v + m * q) - cxx)
            low[0, rows, :] = g0.astype(BF16)
            low[1, rows, :] = (-(k4 * w) * l1).astype(BF16)
            low[2, rows, :] = (kc * l2 - com * cx).astype(BF16)
            low[3, rows, :] = (kc * l3).astype(BF16)
            low[4, rows, :] = (com * w).astype(BF16)
            minus = (-(com * cw)).astype(BF16)
            low[5, rows, :] = minus
            low[6, rows, :] = minus
            return (carry[0] + fold(g0), carry[1] + fold(cot * t))

        sum4, sum5 = lax.fori_loop(0, steps, first, (zero, zero), unroll=UNROLL)
        flat = self.streams[...].reshape(7 * self.count, columns)
        flat_low = low[...].reshape(7 * self.count, columns)
        grad_out(
            lax.dot_general(
                flat, flat_low, (((0,), (0,)), ((), ())), preferred_element_type=F32
            )
        )
        self.layers[...] = lax.dot_general(
            flat_low, self.weights(), (((1,), (1,)), ((), ())), preferred_element_type=F32
        ).reshape(7, self.count, columns)

        def second(step, carry):
            rows = rows_of(step)
            h = self.hidden[rows, :]
            i = [self.layers[j, rows, :] for j in range(7)]
            h2 = h * h
            g = 1.0 - h2
            s = -2.0 * h * g
            lin = i[1] * scaled[0] + i[2] * scaled[1] + i[3] * scaled[2]
            quad = i[4] * squares[0] + i[5] * squares[1] + i[6] * squares[2]
            da = g * (i[0] - 2.0 * h * lin + (6.0 * h2 - 2.0) * quad)
            terms = [
                da,
                da * self.col("t", step),
                da * self.col("x", step),
                da * self.col("y", step),
            ]
            terms += [g * i[1 + d] for d in range(3)] + [s * i[4 + d] for d in range(3)]
            return tuple(c + fold(x) for c, x in zip(carry, terms))

        sums = lax.fori_loop(0, steps, second, (zero,) * 10, unroll=UNROLL)
        sums = [jnp.sum(x, axis=0, keepdims=True) for x in sums]
        rows = [
            sums[1 + d]
            + self.factors[d] * sums[4 + d]
            + 2.0 * self.factors[d] * scaled[d] * sums[7 + d]
            for d in range(3)
        ]
        rows.append(sums[0])
        rows.append(jnp.sum(sum4, axis=0, keepdims=True))
        rows.append(jnp.sum(sum5, axis=0, keepdims=True) * norm)
        for j, row in enumerate(rows):
            edge_out(j, row)


def row_tile(tile):
    return tile.T[0:8, :]


def column_tile(row):
    return jnp.broadcast_to(row, (row.shape[1], row.shape[1])).T


def kernel(
    S, B, CB, FD, points_ref, source_ref, speed_ref, live_ref, index_ref, fh_ref, fe_ref, ch_ref,
    ce_ref, res_out, fg, fge_out, zg, cge_out,
    cedge, fedge, rows_sc, cols, idx_sc, pick_t, pts, lsend, lrecv,
    totals, ltotals, cback, crecv, lback, lcr, cotr, cotc, lcots, lcotr, lcotc,
    st, layers, hid, stl, ll, hl, grads, gh, gr, cge, cge_r, fge, fge_r,
    csum, zst, zr, cez, fown, fst, fxr, fex,
    p_send, p_recv, chip_send, chip_recv, x_send, x_recv, z_send, z_recv, g_send, g_recv,
):
    C = CB * B
    PS = S // CB
    NP = points_ref.shape[1]
    cap = index_ref.shape[1]
    H = fh_ref.shape[1]
    s, b, r = lax.axis_index("sub"), lax.axis_index("blk"), lax.axis_index("rep")
    other = 1 - r
    right, left = lax.rem(s + 1, S), lax.rem(s + S - 1, S)
    peers = [lax.rem(b + d, B) for d in range(1, B)]
    cell = s // max(S // C, 1)
    half_width = float(FD * S) / float(C)
    start = s.astype(F32) * FD

    barrier = pltpu.get_barrier_semaphore()
    pl.semaphore_signal(barrier, inc=1, device_id={"rep": other}, device_id_type=MESH)
    for to in peers:
        pl.semaphore_signal(barrier, inc=1, device_id={"blk": to}, device_id_type=MESH)
    for d in range(1, S):
        pl.semaphore_signal(
            barrier, inc=1, device_id={"sub": lax.rem(s + d, S)}, device_id_type=MESH
        )

    fields = jnp.concatenate(
        [points_ref[...], speed_ref[...], jnp.zeros((4, NP), F32)], axis=0
    )
    pts[b] = fields
    x_rows = lax.broadcasted_iota(jnp.int32, (8, 128), 0) == 1
    idx_sc[...] = jnp.full_like(idx_sc, -1)
    for n in range(2):
        idx_sc[n : n + 1, 0:cap] = index_ref[n : n + 1, :]
        pick_t[n] = (
            lax.broadcasted_iota(jnp.int32, (NP, 128), 0) == idx_sc[n : n + 1, :]
        ).astype(F32)
        listed = jnp.dot(fields, pick_t[n], preferred_element_type=F32, precision=EXACT)
        centre = start - 0.5 if n == 0 else start + (FD + 0.5)
        lsend[n] = listed - jnp.where(x_rows, centre, 0.0)
    pl.semaphore_wait(barrier, S + B - 1)

    def remote(src, dst, send, recv, **where):
        copy = pltpu.make_async_remote_copy(
            src_ref=src, dst_ref=dst, send_sem=send, recv_sem=recv,
            device_id=where, device_id_type=MESH,
        )
        copy.start()
        return copy

    def to_sides(src, dst, at):
        return [
            remote(src.at[0], dst.at[1], p_send.at[at], p_recv.at[at], sub=left),
            remote(src.at[1], dst.at[0], p_send.at[at + 1], p_recv.at[at + 1], sub=right),
        ]

    def to_peers(src_at, dst, at):
        return [
            remote(src_at(to), dst.at[b], p_send.at[at + d], p_recv.at[at + d], blk=to)
            for d, to in enumerate(peers)
        ]

    lists_in = to_sides(lsend, lrecv, 0)
    points_in = to_peers(lambda to: pts.at[b], pts, 6)

    fine_edges = fe_ref[...].astype(F32)
    coarse_edges = ce_ref[...].astype(F32)
    for j in range(6):
        for k in range(FD):
            fedge[k, j : j + 1, :] = fine_edges[j][k : k + 1]
        for k in range(CB):
            cedge[k, j : j + 1, :] = coarse_edges[j][k : k + 1]

    fine_f = (2.0, 2.0, 2.0)
    coarse_f = (2.0, 2.0 / half_width, 2.0)

    def put(at, group):
        for j, row in enumerate(group):
            rows_sc[at + j : at + j + 1, :] = row
        return {"t": 0, "y": 1, "x": at, "w": at + 1, "cw": at + 2, "cx": at + 3, "cxx": at + 4}

    def time_and_y(block):
        rows_sc[0:1, :] = 2.0 * (block[0:1] - 0.5)
        rows_sc[1:2, :] = 2.0 * (block[2:3] - 0.5)

    def fine_rows(at, block, centre):
        dx = block[1:2] - centre
        return put(at, [2.0 * dx, *window_rows(dx, WIDTH_SQ, block[3:4])])

    def coarse_rows(at, block, k):
        shift = lax.rem(b * CB + k - cell + 1 + C, C)
        used = jnp.where(shift < 3, 1.0, 0.0).astype(F32)
        dx = block[1:2] - (cell.astype(F32) + (shift.astype(F32) - 0.5)) * half_width
        window = window_rows(dx, WIDTH_SQ * half_width * half_width, block[3:4])
        return put(at, [2.0 * dx / half_width, *(used * row for row in window)])

    rows_sc[...] = jnp.zeros_like(rows_sc)
    totals[...] = jnp.zeros_like(totals)
    ltotals[...] = jnp.zeros_like(ltotals)

    def coarse_net(place, k, ids):
        at = FD + place * CB + k
        return Net(NP, coarse_f, lambda: cedge[k], lambda: ch_ref[k], cols.at[place], 0, ids,
                   st.at[at], layers.at[at], hid.at[at])

    time_and_y(fields)
    fine_ids = [fine_rows(2 + 5 * k, fields, start + (k + 0.5)) for k in range(FD)]
    coarse_ids = [coarse_rows(2 + 5 * (FD + k), fields, k) for k in range(CB)]
    cols[0] = rows_sc[...].T
    fine = [
        Net(NP, fine_f, lambda k=k: fedge[k], lambda k=k: fh_ref[k], cols.at[0], 0,
            fine_ids[k], st.at[k], layers.at[k], hid.at[k])
        for k in range(FD)
    ]
    coarse = [[coarse_net(0, k, coarse_ids[k]) for k in range(CB)]]
    for net in fine:
        net.forward(totals.at[0])

    for copy in points_in:
        copy.wait()
    for d, source in enumerate(peers):
        block = pts[source]
        time_and_y(block)
        ids = [coarse_rows(2 + 5 * k, block, k) for k in range(CB)]
        cols[1 + d] = rows_sc[...].T
        nets = [coarse_net(1 + d, k, ids[k]) for k in range(CB)]
        coarse.append(nets)
        for net in nets:
            net.forward(totals.at[1 + d])
        cback[source] = row_tile(totals[1 + d])
    coarse_back = to_peers(lambda to: cback.at[to], crecv, 6 + B)

    for copy in lists_in:
        copy.wait()
    lists = []
    for n, k in ((0, 0), (1, FD - 1)):
        block = lrecv[n]
        time_and_y(block)
        ids = fine_rows(2, block, 0.0)
        cols[B + n] = rows_sc[...].T
        net = Net(cap, fine_f, lambda k=k: fedge[k], lambda k=k: fh_ref[k], cols.at[B + n], 0,
                  ids, stl.at[n], ll.at[n], hl.at[n])
        lists.append(net)
        net.forward(ltotals.at[n])
        lback[n] = row_tile(ltotals[n])
    lists_back = to_sides(lback, lcr, 2)

    for net in coarse[0]:
        net.forward(totals.at[0])
    total = row_tile(totals[0])
    for copy in coarse_back + lists_back:
        copy.wait()
    for source in peers:
        total = total + crecv[source]
    for n in range(2):
        total = total + lax.dot_general(
            lcr[n], pick_t[n], (((1,), (1,)), ((), ())), preferred_element_type=F32,
            precision=EXACT,
        )
    count = live_ref[0]
    live = (lax.broadcasted_iota(jnp.int32, (1, NP), 1) < count).astype(F32)
    residual = (total[0:1] * 0.125 - source_ref[...]) * live
    res_out[...] = residual
    cot = residual * 0.125
    loss = jnp.broadcast_to(jnp.sum(residual * residual, axis=1, keepdims=True), (1, NP))
    counted = jnp.full((1, NP), 1.0, F32) * count.astype(F32)
    cotr[b] = jnp.concatenate([cot, loss, counted, jnp.zeros((5, NP), F32)], axis=0)
    cot8 = jnp.broadcast_to(cot, (8, NP))
    for n in range(2):
        lcots[n] = jnp.dot(cot8, pick_t[n], preferred_element_type=F32, precision=EXACT)
    lists_cot = to_sides(lcots, lcotr, 4)
    peers_cot = to_peers(lambda to: cotr.at[b], cotr, 6 + 2 * B)
    cotc[0] = column_tile(cot)
    cge[...] = jnp.zeros_like(cge)
    fge[...] = jnp.zeros_like(fge)

    def run_back(e, net, cotangent, edge_ref, k, more):
        def keep(value):
            value = value.reshape(gh.shape[1:])
            gh[e] = gh[e] + value if more else value

        def keep_edge(j, row):
            edge_ref[k, j : j + 1, :] = edge_ref[k, j : j + 1, :] + row

        net.backward(cotangent, grads, keep, keep_edge)

    def to_core(e):
        return remote(gh.at[e, other], gr.at[e], chip_send.at[e], chip_recv.at[e], rep=other)

    NE = CB + FD
    chip = {}
    for k in range(CB):
        run_back(k, coarse[0][k], cotc.at[0], cge, k, False)
    for copy in peers_cot:
        copy.wait()
    for d, source in enumerate(peers):
        cotc[1 + d] = column_tile(cotr[source, 0:1, :])
    for k in range(CB):
        for d in range(B - 1):
            run_back(k, coarse[1 + d][k], cotc.at[1 + d], cge, k, True)
        chip[k] = to_core(k)
    sums = cotr[0]
    for q in range(1, B):
        sums = sums + cotr[q]
    cge[0, 6:8, :] = wide(sums[1:3], H)
    chip["ce"] = remote(cge, cge_r, chip_send.at[NE], chip_recv.at[NE], rep=other)

    run_back(CB, fine[0], cotc.at[0], fge, 0, False)

    cz = []
    for k in range(CB):
        chip[k].wait()
        value = (gh[k, r] + gr[k]).reshape(csum.shape[1:])
        csum[k] = value
        zst[k] = value.astype(zst.dtype)
    for d in range(1, S):
        to = lax.rem(s + d, S)
        cz.append(
            remote(zst.at[to // PS, lax.rem(to, PS)], zr.at[s], z_send.at[d, 0],
                   z_recv.at[d, 0], sub=to)
        )
    chip["ce"].wait()
    cez[s] = cge[...] + cge_r[...]
    for d in range(1, S):
        to = lax.rem(s + d, S)
        cz.append(remote(cez.at[s], cez.at[s], z_send.at[d, 1], z_recv.at[d, 1], sub=to))

    for k in range(1, FD):
        run_back(CB + k, fine[k], cotc.at[0], fge, k, False)
    for copy in lists_cot:
        copy.wait()
    for n, k in ((0, 0), (1, FD - 1)):
        lcotc[n] = column_tile(lcotr[n, 0:1, :])
        run_back(CB + k, lists[n], lcotc.at[n], fge, k, True)
    for k in range(FD):
        chip[CB + k] = to_core(CB + k)
    chip["fe"] = remote(fge, fge_r, chip_send.at[NE + 1], chip_recv.at[NE + 1], rep=other)

    fx = []
    for k in range(FD):
        chip[CB + k].wait()
        fown[k] = gh[CB + k, r, b] + gr[CB + k, b]
        for d, to in enumerate(peers):
            fst[to, k] = (gh[CB + k, r, to] + gr[CB + k, to]).astype(BF16)
    for d, to in enumerate(peers):
        fx.append(remote(fst.at[to], fxr.at[b], x_send.at[d, 0], x_recv.at[d, 0], blk=to))
    chip["fe"].wait()
    fex[b] = fge[...] + fge_r[...]
    for d, to in enumerate(peers):
        fx.append(remote(fex.at[b], fex.at[b], x_send.at[d, 1], x_recv.at[d, 1], blk=to))

    for copy in cz:
        copy.wait()
    piece = csum[s // PS, lax.rem(s, PS)]
    for d in range(1, S):
        piece = piece + zr[lax.rem(s + d, S)].astype(F32)
    zg[r, s] = piece.astype(zg.dtype)
    cg = []
    for d in range(1, S):
        to = lax.rem(s + d, S)
        cg.append(remote(zg.at[r, s], zg.at[r, s], z_send.at[d, 2], z_recv.at[d, 2], sub=to))
    last = [remote(zg.at[r, s], zg.at[r, s], z_send.at[0, 0], z_recv.at[0, 0], rep=other)]
    edge_sum = cez[0]
    for d in range(1, S):
        edge_sum = edge_sum + cez[d]
    cge_out[...] = edge_sum

    for copy in fx:
        copy.wait()
    for k in range(FD):
        value = fown[k]
        for source in peers:
            value = value + fxr[source, k].astype(F32)
        fg[r, b, k] = value.astype(BF16)
    fgc = [
        remote(fg.at[r, b], fg.at[r, b], g_send.at[1 + d], g_recv.at[1 + d], blk=to)
        for d, to in enumerate(peers)
    ]
    last.append(remote(fg.at[r, b], fg.at[r, b], g_send.at[0], g_recv.at[0], rep=other))
    edge_sum = fex[0]
    for q in range(1, B):
        edge_sum = edge_sum + fex[q]
    fge_out[...] = edge_sum

    for d in range(B - 1):
        fgc[d].wait()
        source = lax.rem(b + B - 1 - d, B)
        last.append(
            remote(fg.at[r, source], fg.at[r, source], g_send.at[B + d], g_recv.at[B + d],
                   rep=other)
        )
    for d in range(1, S):
        cg[d - 1].wait()
        source = lax.rem(s + S - d, S)
        last.append(
            remote(zg.at[r, source], zg.at[r, source], z_send.at[d, 3], z_recv.at[d, 3],
                   rep=other)
        )
    for copy in last:
        copy.wait()


def finish(res_in, fg, fe, zg, ce, res_out, fgh_out, fge_out, cgh_out, cge_out, loss_out):
    B, FD = fg.shape[1], fg.shape[2]
    S, CB = zg.shape[1], ce.shape[0]
    PS = S // CB
    res_out[...] = res_in[...]
    for half in range(2):
        for q in range(B):
            for k in range(FD):
                fgh_out[k, half, q] = fg[half, q, k].astype(F32)
        for p in range(S):
            cgh_out[p // PS, half, p % PS] = zg[half, p].astype(F32)
    for j in range(6):
        for k in range(FD):
            fge_out[j, k : k + 1, :] = fe[k, j : j + 1, :]
        for k in range(CB):
            cge_out[j, k : k + 1, :] = ce[k, j : j + 1, :]
    loss = ce[0, 6:7, 0:128] / ce[0, 7:8, 0:128]
    loss_out[0] = loss[0, 0]


def shards(points, source, speed, live_count, index, fine_hidden, fine_edge, coarse_hidden,
           coarse_edge):
    S, B = lax.axis_size("sub"), lax.axis_size("blk")
    NP = points.shape[1]
    FD, H = fine_hidden.shape[0], fine_hidden.shape[1]
    CB = coarse_hidden.shape[0]
    PS = S // CB
    cap = index.shape[1]
    half = H // 2
    Q = half // B
    RP = half // PS
    wire = BF16 if RP % 16 == 0 else F32
    NE = FD + CB
    NN = FD + B * CB
    vm, dma = pltpu.VMEM, pltpu.SemaphoreType.DMA
    scratch = [
        vm((CB, 8, H), F32), vm((FD, 8, H), F32), vm((128, NP), F32), vm((B + 2, NP, 128), F32),
        vm((8, 128), jnp.int32), vm((2, NP, 128), F32), vm((B, 8, NP), F32),
        vm((2, 8, 128), F32), vm((2, 8, 128), F32),
        vm((B, NP, 128), F32), vm((2, NP, 128), F32), vm((B, 8, NP), F32), vm((B, 8, NP), F32),
        vm((2, 8, NP), F32), vm((2, 8, NP), F32), vm((B, 8, NP), F32), vm((B, NP, 128), F32),
        vm((2, 8, 128), F32), vm((2, 8, 128), F32), vm((2, NP, 128), F32),
        vm((NN, 7, NP, H), BF16), vm((NN, 7, NP, H), F32), vm((NN, NP, H), F32),
        vm((2, 7, cap, H), BF16), vm((2, 7, cap, H), F32), vm((2, cap, H), F32),
        vm((7, NP, H), BF16),
        vm((NE, 2, B, Q, H), F32), vm((NE, B, Q, H), F32),
        vm((CB, 8, H), F32), vm((CB, 8, H), F32), vm((FD, 8, H), F32), vm((FD, 8, H), F32),
        vm((CB, PS, RP, H), F32), vm((CB, PS, RP, H), wire), vm((S, RP, H), wire),
        vm((S, CB, 8, H), F32),
        vm((FD, Q, H), F32), vm((B, FD, Q, H), BF16), vm((B, FD, Q, H), BF16),
        vm((B, FD, 8, H), F32),
        dma((6 + 3 * B,)), dma((6 + 3 * B,)), dma((NE + 2,)), dma((NE + 2,)),
        dma((B, 2)), dma((B, 2)), dma((S, 4)), dma((S, 4)), dma((2 * B,)), dma((2 * B,)),
    ]
    space = pl.BlockSpec(memory_space=pltpu.VMEM)
    scalar = pl.BlockSpec(memory_space=pltpu.SMEM)
    shape = jax.ShapeDtypeStruct
    parts = pl.pallas_call(
        functools.partial(kernel, S, B, CB, FD),
        out_shape=(
            shape((1, NP), F32),
            shape((2, B, FD, Q, H), BF16),
            shape((FD, 8, H), F32),
            shape((2, S, RP, H), wire),
            shape((CB, 8, H), F32),
        ),
        in_specs=[space] * 3 + [scalar] + [space] * 5,
        out_specs=(space,) * 5,
        scratch_shapes=scratch,
        compiler_params=pltpu.CompilerParams(
            collective_id=0, has_side_effects=True, vmem_limit_bytes=56 * 1024 * 1024
        ),
    )(
        points, source.reshape(1, NP), speed.reshape(1, NP), live_count, index,
        fine_hidden, fine_edge.transpose(1, 0, 2), coarse_hidden, coarse_edge.transpose(1, 0, 2),
    )
    outs = pl.pallas_call(
        finish,
        out_shape=(
            shape((1, NP), F32),
            shape((FD, 2, B, Q, H), F32),
            shape((6, FD, H), F32),
            shape((CB, 2, PS, RP, H), F32),
            shape((6, CB, H), F32),
            shape((1,), F32),
        ),
        in_specs=[space] * 5,
        out_specs=(space,) * 5 + (scalar,),
        compiler_params=pltpu.CompilerParams(vmem_limit_bytes=60 * 1024 * 1024),
    )(*parts)
    return (
        outs[0].reshape(NP), outs[1].reshape(FD, H, H), outs[2].transpose(1, 0, 2),
        outs[3].reshape(CB, H, H), outs[4].transpose(1, 0, 2), outs[5],
    )


def solution(mesh):
    return jax.shard_map(
        shards,
        mesh=mesh,
        in_specs=(
            P(None, ("groups", "sub", "blk", "rep")),
            P(("groups", "sub", "blk", "rep")),
            P(("groups", "sub", "blk", "rep")),
            P(("groups", "sub", "blk", "rep")),
            P(None, ("groups", "sub", "blk", "rep")),
            P("sub", None, None),
            P("sub", None, None),
            P("blk", None, None),
            P("blk", None, None),
        ),
        out_specs=(
            P(("groups", "sub", "blk", "rep")),
            P(("groups", "sub"), None, None),
            P(("groups", "sub"), None, None),
            P(("groups", "blk"), None, None),
            P(("groups", "blk"), None, None),
            P("groups"),
        ),
        check_vma=False,
    )
```
